32 devices in a mesh: grp: 2 (over x), row: 8 (over z, y), col: 2 (over core).
Axes of the slice: x: 2, y: 2, z: 4, core: 2. Of those that a mesh axis runs over, the one named last changes fastest.
Arguments:
- a_tiles: bfloat16 [32768, 2048], P(('grp', 'row'), 'col'), parts along dimension 0, may hold values from -6 to 6
- b_tiles: bfloat16 [4096, 4096], P(('grp', 'row'), 'col'), parts along dimension 0, may hold values from -0.125 to 0.125
- a_mask: int32 [128, 8], P('grp'), parts along dimension 0, may hold values from 0 to 1, as said below
- b_mask: int32 [16, 16], P('grp'), parts along dimension 0, may hold values 0 or 1
- c_given: bfloat16 [32768, 4096], P(('grp', 'row'), 'col'), parts along dimension 0, may hold values from -6 to 6
Outputs:
- c_result: bfloat16 [32768, 4096], P(('grp', 'row'), 'col'), parts along dimension 0
The draws below stay inside these ranges and needn't reach their ends.
There are 2 independent parts, one for each index of `grp`. The reference program is written for one: setup_inputs(seed, part) draws one part's arguments, and reference() takes and returns one part's arrays. A program takes and returns all parts, laid end to end along the dimension named above; each array names one. Nothing has to cross between parts.
Inputs may be any that keep to these rules, and one draw needn't show every extreme that they name: `a_mask`: 1 where tile (i, k) of a_tiles is kept, else 0; the share of ones differs between tile rows. `b_mask`: 1 where tile (k, j) of b_tiles is kept, else 0.
All inputs are finite; a program needn't handle non-finite values.
Results may differ from the reference program's by a relative error of at most 0.001.
Values may be sent and summed in bfloat16 or wider, within the bound.
No kernel may reach another device: no remote copies, remote signals or barrier semaphores. Data moves between devices by JAX's collectives and lax.ppermute only.
A program may use at most 192 MiB of HBM per device.

```python
import jax
import jax.numpy as jnp

STEPS = 8
M = 16384
N = 4096
K = 2048
MT = 64
NT = 16


def draw_a_mask(key, part):
    key = jax.random.fold_in(key, 11)
    first_key, second_key = jax.random.split(key)
    levels = jax.random.randint(first_key, (MT, 1), 1, 8)
    cells = jax.random.randint(second_key, (MT, STEPS), 0, 8)
    return (cells < levels).astype(jnp.int32)


def with_ends(result, stream_key, low, largest):
    longest = result.shape.index(max(result.shape))
    spots = []
    for shift in (0, 1):
        where = [jax.random.randint(jax.random.fold_in(stream_key, axis), (), 0, length) for axis, length in enumerate(result.shape)]
        where[longest] = (where[longest] + shift) % result.shape[longest]
        spots.append(tuple(where))
    return result.at[spots[0]].set(low).at[spots[1]].set(largest)


def steps_of(rng, extent, shards, low, largest):
    def one(position, parts):
        steps = jax.random.uniform(jax.random.fold_in(jax.random.fold_in(rng, 6), position), (parts,), jnp.float32, low / len(shards), largest / len(shards))
        return jnp.repeat(jnp.exp(steps), extent[position] // parts).reshape((-1,) + (1,) * (len(extent) - position - 1))

    loudness = one(*shards[0])
    for cut in shards[1:]:
        loudness = loudness * one(*cut)
    return loudness


def centred(rng, shape, width, bound, pieces=(), kind=jnp.bfloat16):
    array = width * jax.random.normal(rng, shape, jnp.float32)
    if pieces:
        array = array * steps_of(rng, shape, pieces, -0.22, 0.18)
    return jnp.clip(array, -bound, bound).astype(kind)


def setup_inputs(seed: int = 0, part: int = 0) -> dict:
    arg_keys = jax.random.split(jax.random.key(seed), 6)
    part_splits = jax.random.split(jax.random.fold_in(arg_keys[5], part), 6)
    a_tiles = centred(part_splits[0], (M, K), 1.0, 6.0, ((0, 8), (1, 2)))
    b_tiles = centred(part_splits[1], (K, N), K ** -0.5, 0.125, ((0, 8), (1, 2)))
    a_mask = draw_a_mask(jax.random.fold_in(jax.random.fold_in(arg_keys[5], part), 71), part)
    b_mask = with_ends((jax.random.randint(part_splits[3], (STEPS, NT), 0, 4) < 3).astype(jnp.int32), jax.random.fold_in(part_splits[3], 1), 0, 1)
    c_given = centred(part_splits[4], (M, N), 1.0, 6.0, ((0, 8), (1, 2)))
    return dict(a_tiles=a_tiles, b_tiles=b_tiles, a_mask=a_mask, b_mask=b_mask, c_given=c_given)


def expand(source, flags):
    row_count, col_count = source.shape
    tile_rows, tile_cols = flags.shape
    shaped = source.reshape(tile_rows, row_count // tile_rows, tile_cols, col_count // tile_cols)
    kept = shaped * flags[:, None, :, None].astype(source.dtype)
    return kept.reshape(row_count, col_count)


def reference(a_tiles, b_tiles, a_mask, b_mask, c_given):
    a_kept = expand(a_tiles, a_mask)
    b_kept = expand(b_tiles, b_mask)
    product = jnp.dot(a_kept, b_kept, preferred_element_type=jnp.float32)
    return (c_given.astype(jnp.float32) + product).astype(jnp.bfloat16)
```

```python
import functools

import jax
import jax.numpy as jnp
from jax import lax
from jax.experimental import pallas as pl
from jax.experimental.pallas import tpu as pltpu
from jax.sharding import PartitionSpec as P

TW = 256
PANEL = 512
ROWS = 256


def ring_of(n):
    if n == 8:
        return [0, 2, 4, 6, 7, 5, 3, 1]
    return list(range(n))


def body(place, a_mask, b_mask, *refs, offsets, panel, first_row, base_wide, out_wide, chained):
    count = len(offsets)
    own_ref, other_ref = refs[:2]
    blocks = refs[2 : 2 + count]
    base_ref = refs[2 + count]
    out_ref, parts, total = refs[3 + count + chained :]
    step = pl.program_id(0)
    depth = blocks[0].shape[0]
    half = own_ref.shape[1]
    per_half = half // depth
    for index in range(per_half):
        parts[index] = own_ref[:, index * depth : (index + 1) * depth]
        parts[per_half + index] = other_ref[:, index * depth : (index + 1) * depth]
    total[...] = base_ref[...].astype(jnp.float32)
    tile_row = place[0] + first_row // TW + step * (ROWS // TW)
    for slot, offset in enumerate(offsets):
        owner = place[2 + offset]
        tile_k = owner * depth // TW
        where = lax.rem(owner + (2 - place[1]) * per_half, 2 * per_half)
        for j in range(PANEL // TW):
            flag = a_mask[tile_row, tile_k] * b_mask[tile_k, place[1] * 8 + panel * (PANEL // TW) + j]

            @pl.when(flag != 0)
            def _():
                total[:, j * TW : (j + 1) * TW] += jnp.dot(
                    parts[where],
                    blocks[slot][:, j * TW : (j + 1) * TW],
                    preferred_element_type=jnp.float32,
                )

    out_ref[...] = total[...].astype(out_ref.dtype)


def multiply(place, a_mask, b_mask, own, other, blocks, base, out, *, panel, first_row, row_count, base_wide, out_wide, width):
    offsets = tuple(sorted(blocks))
    height = own.shape[0]
    skip = first_row // ROWS
    arrays, specs = [], []
    for offset in offsets:
        array = blocks[offset]
        arrays.append(array)
        column = panel if array.shape[1] != PANEL else 0
        specs.append(pl.BlockSpec((array.shape[0], PANEL), functools.partial(lambda c, i, *_: (0, c), column)))
    depth = arrays[0].shape[0]
    base_column = 0 if base_wide else panel
    in_specs = [
        pl.BlockSpec((ROWS, own.shape[1]), lambda i, *_: (i + skip, 0)),
        pl.BlockSpec((ROWS, own.shape[1]), lambda i, *_: (i + skip, 0)),
        *specs,
        pl.BlockSpec((ROWS, PANEL), lambda i, *_: (i + (0 if base_wide else skip), base_column)),
    ]
    operands = [place, a_mask, b_mask, own, other, *arrays, base]
    aliases = {}
    if out_wide:
        out_shape = jax.ShapeDtypeStruct((row_count, PANEL), jnp.float32)
        out_spec = pl.BlockSpec((ROWS, PANEL), lambda i, *_: (i, 0))
    else:
        out_shape = jax.ShapeDtypeStruct((height, width), jnp.bfloat16)
        out_spec = pl.BlockSpec((ROWS, PANEL), lambda i, *_: (i + skip, panel))
    chained = out is not None
    if chained:
        aliases = {len(operands): 0}
        operands.append(out)
        in_specs.append(pl.BlockSpec(memory_space=pl.ANY))
    flops = 2 * row_count * PANEL * depth * len(offsets)
    return pl.pallas_call(
        functools.partial(
            body, offsets=offsets, panel=panel, first_row=first_row, base_wide=base_wide, out_wide=out_wide, chained=chained
        ),
        grid_spec=pltpu.PrefetchScalarGridSpec(
            num_scalar_prefetch=3,
            grid=(row_count // ROWS,),
            in_specs=in_specs,
            out_specs=out_spec,
            scratch_shapes=[
                pltpu.VMEM((2 * own.shape[1] // depth, ROWS, depth), jnp.bfloat16),
                pltpu.VMEM((ROWS, PANEL), jnp.float32),
            ],
        ),
        out_shape=out_shape,
        input_output_aliases=aliases,
        cost_estimate=pl.CostEstimate(flops=flops, bytes_accessed=row_count * 6000, transcendentals=0),
        compiler_params=pltpu.CompilerParams(vmem_limit_bytes=24 * 1024 * 1024),
    )(*operands)


def on_device(n, a_tiles, b_tiles, a_mask, b_mask, c_given):
    ring = ring_of(n)
    right = [(ring[i], ring[(i + 1) % n]) for i in range(n)]
    left = [(t, s) for s, t in right]
    row = lax.axis_index("row")
    col = lax.axis_index("col")
    height, width = c_given.shape
    far = n // 2

    b_panels = [b_tiles[:, p * PANEL : (p + 1) * PANEL] for p in range(width // PANEL)]
    blocks = [{0: b_tiles} for _ in b_panels]
    other = None
    for first in range(0, len(b_panels), 2):
        for hop in range(1, far + 1):
            for which in range(2):
                p = first + which
                for sign, pairs, keep in ((-1, right, 0), (1, left, 1)):
                    if hop == far and which != keep:
                        continue
                    p = first + (which if sign < 0 else 1 - which)
                    if hop == far:
                        p = first + keep
                    source = b_panels[p] if hop == 1 else blocks[p][sign * (hop - 1)]
                    blocks[p][sign * hop] = lax.ppermute(source, "row", pairs)
        if other is None:
            other = lax.ppermute(a_tiles, "col", [(0, 1), (1, 0)])

    ring_array = jnp.array(ring, jnp.int32)
    position = jnp.argmax(ring_array == row).astype(jnp.int32)
    owners = ring_array[(position + jnp.arange(n, dtype=jnp.int32)) % n]
    place = jnp.concatenate([jnp.stack([row * (height // TW), col]).astype(jnp.int32), owners])

    def shift(table):
        return {(offset if offset >= 0 else n + offset): array for offset, array in table.items()}

    call = functools.partial(multiply, place, a_mask, b_mask, a_tiles, other, width=width)
    out = None
    half = height // 2
    for p in range(len(b_panels)):
        last = p >= len(b_panels) - 2
        table = shift(blocks[p])
        for first_row in (0, half):
            settings = dict(panel=p, first_row=first_row, row_count=half)
            if not last:
                out = call(table, c_given, out, base_wide=False, out_wide=False, **settings)
                continue
            early = {k: v for k, v in table.items() if k != far}
            wide = call(early, c_given, None, base_wide=False, out_wide=True, **settings)
            out = call({far: table[far]}, wide, out, base_wide=True, out_wide=False, **settings)
    return out


def solution(mesh):
    return jax.shard_map(
        functools.partial(on_device, mesh.shape["row"]),
        mesh=mesh,
        in_specs=(
            P(("grp", "row"), "col"),
            P(("grp", "row"), "col"),
            P("grp", None),
            P("grp", None),
            P(("grp", "row"), "col"),
        ),
        out_specs=P(("grp", "row"), "col"),
        check_vma=False,
    )
```

```python
import collections
import functools

import jax
import jax.numpy as jnp
from jax import lax
from jax.experimental import pallas as pl
from jax.experimental.pallas import tpu as pltpu
from jax.sharding import PartitionSpec as P

TW = 256
ROWS = 512
MIB = 1024 * 1024
VMEM = 20 * MIB


def ring_of(n):
    if n == 8:
        return [0, 2, 4, 6, 7, 5, 3, 1]
    return list(range(n))


def prepare_body(place, a_mask, own_ref, other_ref, out_ref, *, depth, n):
    per_half = n // 2
    tiles = own_ref.shape[0] // TW
    for tile in range(tiles):
        rows = slice(tile * TW, (tile + 1) * TW)
        tile_row = place[0] + pl.program_id(0) * tiles + tile
        for away, ref in enumerate((own_ref, other_ref)):
            first = lax.rem(place[1] + away, 2) * per_half
            for index in range(per_half):
                owner = first + index
                flag = a_mask[tile_row, owner * depth // TW].astype(out_ref.dtype)
                out_ref[place[2 + n + owner], rows, :] = ref[rows, index * depth : (index + 1) * depth] * flag


def prepare(place, a_mask, own, other, n):
    height, half = own.shape
    depth = 2 * half // n
    return pl.pallas_call(
        functools.partial(prepare_body, depth=depth, n=n),
        grid_spec=pltpu.PrefetchScalarGridSpec(
            num_scalar_prefetch=2,
            grid=(height // ROWS,),
            in_specs=[pl.BlockSpec((ROWS, half), lambda i, *_: (i, 0))] * 2,
            out_specs=pl.BlockSpec((n, ROWS, depth), lambda i, *_: (0, i, 0)),
        ),
        out_shape=pltpu.VMEM((n, height, depth), jnp.bfloat16),
        cost_estimate=pl.CostEstimate(flops=0, bytes_accessed=height * half // 16, transcendentals=0),
        compiler_params=pltpu.CompilerParams(vmem_limit_bytes=VMEM),
    )(place, a_mask, own, other)


def multiply_body(place, b_mask, *refs, layout, low, high, first, chained):
    left, refs = refs[: high - low], refs[high - low :]
    blocks = refs[: len(layout)]
    base_ref = refs[len(layout)]
    out_ref, kept = refs[len(layout) + 1 + chained :]
    depth = blocks[0].shape[0]

    @pl.when(pl.program_id(0) == 0)
    def _():
        for ref, (slot, shift) in zip(blocks, layout):
            tile_k = place[2 + slot] * depth // TW
            for j in range(ref.shape[1] // TW):
                at = shift + j * TW
                flag = b_mask[tile_k, place[1] * 8 + (first + at) // TW].astype(kept.dtype)
                block = ref[:, j * TW : (j + 1) * TW]
                kept[(slot - low) * depth : (slot - low + 1) * depth, at : at + TW] = block * flag

    left = [ref[0] for ref in left]
    left = jnp.concatenate(left, axis=1) if len(left) > 1 else left[0]
    product = jnp.dot(left, kept[...], preferred_element_type=jnp.float32)
    out_ref[...] = (base_ref[...].astype(jnp.float32) + product).astype(out_ref.dtype)


def multiply(place, b_mask, a_kept, arrived, base, base_column, out, *, low, high, first, size, wide, width):
    height = a_kept.shape[1]
    depth = arrived[0][2].shape[0]
    operands = [place, b_mask] + [a_kept] * (high - low)
    whole = pl.BlockSpec(memory_space=pltpu.VMEM)
    in_specs = [
        pl.BlockSpec((1, ROWS, depth), functools.partial(lambda slot, i, *_: (slot, i, 0), slot)) for slot in range(low, high)
    ]
    for _, _, array in arrived:
        operands.append(array)
        if array.shape[1] == width:
            in_specs.append(pl.BlockSpec((depth, size), lambda i, *_: (0, first // size)))
        else:
            in_specs.append(whole)
    operands.append(base)
    in_specs.append(pl.BlockSpec((ROWS, size), lambda i, *_: (i, base_column // size)))
    if wide:
        out_shape = pltpu.VMEM((height, size), jnp.float32)
        out_spec = pl.BlockSpec((ROWS, size), lambda i, *_: (i, 0))
    else:
        out_shape = jax.ShapeDtypeStruct((height, width), jnp.bfloat16)
        out_spec = pl.BlockSpec((ROWS, size), lambda i, *_: (i, first // size))
    aliases = {}
    if out is not None:
        aliases = {len(operands): 0}
        operands.append(pltpu.with_memory_space_constraint(out, pltpu.HBM))
        in_specs.append(pl.BlockSpec(memory_space=pl.ANY))
    extent = (high - low) * depth
    return pl.pallas_call(
        functools.partial(
            multiply_body,
            layout=tuple((slot, shift) for slot, shift, _ in arrived),
            low=low,
            high=high,
            first=first,
            chained=out is not None,
        ),
        grid_spec=pltpu.PrefetchScalarGridSpec(
            num_scalar_prefetch=2,
            grid=(height // ROWS,),
            in_specs=in_specs,
            out_specs=out_spec,
            scratch_shapes=[pltpu.VMEM((extent, size), jnp.bfloat16)],
        ),
        out_shape=out_shape,
        input_output_aliases=aliases,
        cost_estimate=pl.CostEstimate(
            flops=height * size * extent // 16, bytes_accessed=height * size // 16, transcendentals=0
        ),
        compiler_params=pltpu.CompilerParams(vmem_limit_bytes=VMEM),
    )(*operands)


def on_device(n, a_tiles, b_tiles, a_mask, b_mask, c_given):
    ring = ring_of(n)
    right = [(ring[i], ring[(i + 1) % n]) for i in range(n)]
    left = [(t, s) for s, t in right]
    row = lax.axis_index("row")
    col = lax.axis_index("col")
    height, width = c_given.shape
    far = n // 2
    panel = width // 2

    offsets = [0] + [sign * hop for hop in range(1, far) for sign in (-1, 1)] + [far]
    table = []
    for r in range(n):
        owners = [ring[(ring.index(r) + o) % n] for o in offsets]
        table.append(owners + [owners.index(owner) for owner in range(n)])
    table = lax.dynamic_index_in_dim(jnp.array(table, jnp.int32), row, 0, keepdims=False)
    place = jnp.concatenate([jnp.stack([row * (height // TW), col]).astype(jnp.int32), table])

    rounds = [(p, hop, 0, panel) for hop in range(1, far) for p in range(2)]
    rounds += [(0, far, 0, panel), (1, far, 0, panel)]
    work = collections.defaultdict(list)
    last = len(rounds)
    work[last - 4] = [(0, 0, n - 3, 0, panel)]
    work[last - 3] = [(1, 0, n - 3, 0, panel)]
    work[last - 2] = [(0, n - 3, n - 1, 0, panel)]
    work[last] = [(1, n - 3, n - 1, 0, panel), (0, n - 1, n, 0, panel), (1, n - 1, n, 0, panel)]

    blocks = [{0: b_tiles} for _ in range(2)]
    other = a_kept = out = None
    wide = {}
    tied = []
    for index in range(last + 1):
        if index < last:
            p, hop, start, stop = rounds[index]
            sources = []
            for sign in (-1, 1):
                if hop == 1:
                    source = b_tiles[:, p * panel : (p + 1) * panel]
                else:
                    source = blocks[p][sign * (hop - 1)]
                if hop == far:
                    middle = (start + stop) // 2
                    source = source[:, start:middle] if sign < 0 else source[:, middle:stop]
                sources.append(source)
            if tied:
                *sources, _ = lax.optimization_barrier((*sources, tied))
            tied = []
            for sign, pairs, source in zip((-1, 1), (right, left), sources):
                key = (sign * hop, start) if hop == far else sign * hop
                blocks[p][key] = lax.ppermute(source, "row", pairs)
        if index == 0:
            other = lax.ppermute(a_tiles, "col", [(0, 1), (1, 0)])
        if index == 1:
            source = pltpu.with_memory_space_constraint(a_tiles, pltpu.HBM)
            a_kept = prepare(place, a_mask, source, other, n)
            tied.append(a_kept)
        for p, low, high, start, stop in work[index]:
            arrived = []
            for slot in range(low, high):
                if offsets[slot] == far:
                    arrived.append((slot, 0, blocks[p][-far, start]))
                    arrived.append((slot, (stop - start) // 2, blocks[p][far, start]))
                else:
                    arrived.append((slot, 0, blocks[p][offsets[slot]]))
            done = high == n
            if low:
                base, base_column = wide[p], start
            else:
                base, base_column = pltpu.with_memory_space_constraint(c_given, pltpu.HBM), p * panel + start
            result = multiply(
                place, b_mask, a_kept, arrived, base, base_column, out if done else None,
                low=low, high=high, first=p * panel + start, size=stop - start, wide=not done, width=width,
            )
            tied.append(result)
            if done:
                out = result
            else:
                wide[p] = result
    return out


def solution(mesh):
    return jax.shard_map(
        functools.partial(on_device, mesh.shape["row"]),
        mesh=mesh,
        in_specs=(
            P(("grp", "row"), "col"),
            P(("grp", "row"), "col"),
            P("grp", None),
            P("grp", None),
            P(("grp", "row"), "col"),
        ),
        out_specs=P(("grp", "row"), "col"),
        check_vma=False,
    )
```

```python
import collections
import functools

import jax
import jax.numpy as jnp
from jax import lax
from jax.experimental import pallas as pl
from jax.experimental.pallas import tpu as pltpu
from jax.sharding import PartitionSpec as P

TW = 256
ROWS = 512
LAST_ROWS = 1024
MIB = 1024 * 1024
VMEM = 20 * MIB
SEND = 3
GATHER_VMEM = 16 * MIB
STEPS_OF = {False: 2, True: 2}


def ring_of(n):
    if n == 8:
        return [0, 2, 4, 6, 7, 5, 3, 1]
    return list(range(n))


def prepare_body(place, a_mask, own_ref, other_ref, out_ref, *, depth, n):
    per_half = n // 2
    tiles = own_ref.shape[0] // TW
    for tile in range(tiles):
        rows = slice(tile * TW, (tile + 1) * TW)
        tile_row = place[0] + pl.program_id(0) * tiles + tile
        for away, ref in enumerate((own_ref, other_ref)):
            first = lax.rem(place[1] + away, 2) * per_half
            for index in range(per_half):
                owner = first + index
                flag = a_mask[tile_row, owner * depth // TW].astype(out_ref.dtype)
                out_ref[place[2 + n + owner], rows, :] = ref[rows, index * depth : (index + 1) * depth] * flag


def prepare(place, a_mask, own, other, n):
    height, half = own.shape
    depth = 2 * half // n
    return pl.pallas_call(
        functools.partial(prepare_body, depth=depth, n=n),
        grid_spec=pltpu.PrefetchScalarGridSpec(
            num_scalar_prefetch=2,
            grid=(height // ROWS,),
            in_specs=[pl.BlockSpec((ROWS, half), lambda i, *_: (i, 0))] * 2,
            out_specs=pl.BlockSpec((n, ROWS, depth), lambda i, *_: (0, i, 0)),
        ),
        out_shape=pltpu.VMEM((n, height, depth), jnp.bfloat16),
        cost_estimate=pl.CostEstimate(flops=0, bytes_accessed=height * half // 16, transcendentals=0),
        compiler_params=pltpu.CompilerParams(vmem_limit_bytes=VMEM),
    )(place, a_mask, own, other)


def multiply_body(place, b_mask, *refs, layout, low, high, first, chained):
    left, refs = refs[: high - low], refs[high - low :]
    blocks = refs[: len(layout)]
    base_ref = refs[len(layout)]
    out_ref, kept = refs[len(layout) + 1 + chained :]
    depth = blocks[0].shape[0]

    @pl.when(pl.program_id(0) == 0)
    def _():
        for ref, (slot, shift) in zip(blocks, layout):
            tile_k = place[2 + slot] * depth // TW
            for j in range(ref.shape[1] // TW):
                at = shift + j * TW
                flag = b_mask[tile_k, place[1] * 8 + (first + at) // TW].astype(kept.dtype)
                block = ref[:, j * TW : (j + 1) * TW]
                kept[(slot - low) * depth : (slot - low + 1) * depth, at : at + TW] = block * flag

    left = [ref[0] for ref in left]
    left = jnp.concatenate(left, axis=1) if len(left) > 1 else left[0]
    product = jnp.dot(left, kept[...], preferred_element_type=jnp.float32)
    out_ref[...] = (base_ref[...].astype(jnp.float32) + product).astype(out_ref.dtype)


def multiply(place, b_mask, a_kept, arrived, base, base_column, out, *, low, high, first, size, wide, width):
    height = a_kept.shape[1]
    depth = arrived[0][2].shape[0]
    rows = LAST_ROWS if high - low == 1 else ROWS
    operands = [place, b_mask] + [a_kept] * (high - low)
    whole = pl.BlockSpec(memory_space=pltpu.VMEM)
    in_specs = [
        pl.BlockSpec((1, rows, depth), functools.partial(lambda slot, i, *_: (slot, i, 0), slot)) for slot in range(low, high)
    ]
    for _, _, array in arrived:
        operands.append(array)
        if array.shape[1] == width:
            in_specs.append(pl.BlockSpec((depth, size), lambda i, *_: (0, first // size)))
        else:
            in_specs.append(whole)
    operands.append(base)
    in_specs.append(pl.BlockSpec((rows, size), lambda i, *_: (i, base_column // size)))
    if wide:
        out_shape = pltpu.VMEM((height, size), jnp.float32)
        out_spec = pl.BlockSpec((rows, size), lambda i, *_: (i, 0))
    else:
        out_shape = jax.ShapeDtypeStruct((height, width), jnp.bfloat16)
        out_spec = pl.BlockSpec((rows, size), lambda i, *_: (i, first // size))
    aliases = {}
    if out is not None:
        aliases = {len(operands): 0}
        operands.append(pltpu.with_memory_space_constraint(out, pltpu.HBM))
        in_specs.append(pl.BlockSpec(memory_space=pl.ANY))
    extent = (high - low) * depth
    return pl.pallas_call(
        functools.partial(
            multiply_body,
            layout=tuple((slot, shift) for slot, shift, _ in arrived),
            low=low,
            high=high,
            first=first,
            chained=out is not None,
        ),
        grid_spec=pltpu.PrefetchScalarGridSpec(
            num_scalar_prefetch=2,
            grid=(height // rows,),
            in_specs=in_specs,
            out_specs=out_spec,
            scratch_shapes=[pltpu.VMEM((extent, size), jnp.bfloat16)],
        ),
        out_shape=out_shape,
        input_output_aliases=aliases,
        cost_estimate=pl.CostEstimate(
            flops=height * size * extent // 16, bytes_accessed=height * size // 16, transcendentals=0
        ),
        compiler_params=pltpu.CompilerParams(vmem_limit_bytes=VMEM),
    )(*operands)


def places(n, row, col, height):
    ring = ring_of(n)
    far = n // 2
    offsets = [0] + [sign * hop for hop in range(1, far) for sign in (-1, 1)] + [far]
    table = []
    for r in range(n):
        owners = [ring[(ring.index(r) + o) % n] for o in offsets]
        table.append(owners + [owners.index(owner) for owner in range(n)])
    table = lax.dynamic_index_in_dim(jnp.array(table, jnp.int32), row, 0, keepdims=False)
    return offsets, jnp.concatenate([jnp.stack([row * (height // TW), col]).astype(jnp.int32), table])


def dense(n, a_tiles, b_tiles, a_mask, b_mask, c_given):
    ring = ring_of(n)
    right = [(ring[i], ring[(i + 1) % n]) for i in range(n)]
    left = [(t, s) for s, t in right]
    row = lax.axis_index("row")
    col = lax.axis_index("col")
    height, width = c_given.shape
    far = n // 2
    panel = width // 2

    offsets, place = places(n, row, col, height)

    rounds = [(p, hop, 0, panel) for hop in range(1, far) for p in range(2)]
    rounds += [(0, far, 0, panel), (1, far, 0, panel)]
    work = collections.defaultdict(list)
    last = len(rounds)
    work[last - 4] = [(0, 0, n - 3, 0, panel)]
    work[last - 3] = [(1, 0, n - 3, 0, panel)]
    work[last - 2] = [(0, n - 3, n - 1, 0, panel)]
    work[last] = [(1, n - 3, n - 1, 0, panel), (0, n - 1, n, 0, panel), (1, n - 1, n, 0, panel)]

    blocks = [{0: b_tiles} for _ in range(2)]
    other = a_kept = out = None
    wide = {}
    tied = []
    for index in range(last + 1):
        if index < last:
            p, hop, start, stop = rounds[index]
            sources = []
            for sign in (-1, 1):
                if hop == 1:
                    source = b_tiles[:, p * panel : (p + 1) * panel]
                else:
                    source = blocks[p][sign * (hop - 1)]
                if hop == far:
                    middle = (start + stop) // 2
                    source = source[:, start:middle] if sign < 0 else source[:, middle:stop]
                sources.append(source)
            if tied:
                *sources, _ = lax.optimization_barrier((*sources, tied))
            tied = []
            for sign, pairs, source in zip((-1, 1), (right, left), sources):
                key = (sign * hop, start) if hop == far else sign * hop
                blocks[p][key] = lax.ppermute(source, "row", pairs)
        if index == 0:
            other = lax.ppermute(a_tiles, "col", [(0, 1), (1, 0)])
        if index == 1:
            source = pltpu.with_memory_space_constraint(a_tiles, pltpu.HBM)
            a_kept = prepare(place, a_mask, source, other, n)
            tied.append(a_kept)
        for p, low, high, start, stop in work[index]:
            arrived = []
            for slot in range(low, high):
                if offsets[slot] == far:
                    arrived.append((slot, 0, blocks[p][-far, start]))
                    arrived.append((slot, (stop - start) // 2, blocks[p][far, start]))
                else:
                    arrived.append((slot, 0, blocks[p][offsets[slot]]))
            done = high == n
            if low:
                base, base_column = wide[p], start
            else:
                base, base_column = pltpu.with_memory_space_constraint(c_given, pltpu.HBM), p * panel + start
            result = multiply(
                place, b_mask, a_kept, arrived, base, base_column, out if done else None,
                low=low, high=high, first=p * panel + start, size=stop - start, wide=not done, width=width,
            )
            tied.append(result)
            if done:
                out = result
            else:
                wide[p] = result
    return out


def pack_body(b_mask, b_hbm, *refs, n, tiles):
    plan = refs[6]
    rows, (b_ref, arrived) = refs[7:9], refs[9:]
    ring = ring_of(n)
    depth = b_ref.shape[0]
    fetch = pltpu.make_async_copy(b_hbm, b_ref, arrived)
    fetch.start()
    far = n // 2
    need = jnp.int32(0)
    for c in range(2):
        kept = []
        for owner in ring:
            total = jnp.int32(0)
            for j in range(tiles):
                total += b_mask[owner * depth // TW, c * tiles + j]
            kept.append(total)
        span = [jnp.maximum(total, 2 * SEND) for total in kept]
        for q in range(n):
            right = sum(span[(q - hop) % n] for hop in range(1, far))
            left = sum(span[(q + hop) % n] for hop in range(1, far))
            both = lax.shift_right_logical(right + left + kept[(q + far) % n] + 1, 1)
            need = jnp.maximum(need, jnp.maximum(jnp.maximum(right, left), both))
    plan[0] = need

    mine = lax.axis_index("row") * depth // TW
    half = lax.axis_index("col") * tiles
    flags = [b_mask[mine, half + j] for j in range(tiles)]
    total = sum(flags)
    before = jnp.int32(0)
    fetch.wait()
    for j in range(tiles):
        tile = b_ref[:, j * TW : (j + 1) * TW]
        dropped = total + j - before
        rows[0][jnp.where(flags[j] != 0, before, dropped)] = tile
        rows[1][jnp.where(flags[j] != 0, total - 1 - before, dropped)] = tile
        before += flags[j]
    end = jnp.maximum(total, 2 * SEND)
    plan[1] = 3 * SEND - end
    for side in range(2):
        refs[3 * side][...] = rows[side][:SEND]
        refs[3 * side + 1][...] = rows[side][SEND : 2 * SEND]
        for i in range(SEND):
            refs[3 * side + 2][i] = rows[side][end - SEND + i]


def pack(b_mask, b_tiles, n):
    depth, width = b_tiles.shape
    tiles = width // TW
    whole = pl.BlockSpec(memory_space=pltpu.VMEM)
    return pl.pallas_call(
        functools.partial(pack_body, n=n, tiles=tiles),
        grid_spec=pltpu.PrefetchScalarGridSpec(
            num_scalar_prefetch=1,
            grid=(1,),
            in_specs=[pl.BlockSpec(memory_space=pl.ANY)],
            out_specs=[whole] * 6 + [pl.BlockSpec(memory_space=pltpu.SMEM)],
            scratch_shapes=[pltpu.VMEM((tiles, depth, TW), jnp.bfloat16)] * 2
            + [pltpu.VMEM((depth, width), jnp.bfloat16), pltpu.SemaphoreType.DMA],
        ),
        out_shape=[pltpu.VMEM((SEND, depth, TW), jnp.bfloat16)] * 6 + [jax.ShapeDtypeStruct((2,), jnp.int32)],
        compiler_params=pltpu.CompilerParams(vmem_limit_bytes=VMEM),
    )(b_mask, pltpu.with_memory_space_constraint(b_tiles, pltpu.HBM))


def choose_body(plan, *refs, count):
    for before, last, out in (refs[0:2] + refs[4:5], refs[2:4] + refs[5:6]):
        for start in range(1, SEND + 1):

            @pl.when(plan[1] == start)
            def _():
                for i in range(count):
                    at = start + i
                    out[i] = before[at] if at < SEND else last[at - SEND]


def choose(plan, arrays, count):
    shape = (count,) + arrays[0].shape[1:]
    whole = pl.BlockSpec(memory_space=pltpu.VMEM)
    return pl.pallas_call(
        functools.partial(choose_body, count=count),
        grid_spec=pltpu.PrefetchScalarGridSpec(
            num_scalar_prefetch=1, grid=(1,), in_specs=[whole] * 4, out_specs=[whole] * 2
        ),
        out_shape=[pltpu.VMEM(shape, jnp.bfloat16)] * 2,
        cost_estimate=pl.CostEstimate(flops=0, bytes_accessed=1024, transcendentals=0),
        compiler_params=pltpu.CompilerParams(vmem_limit_bytes=VMEM),
    )(plan, *arrays)


def gather_multiply_body(
    place, b_mask, *refs, low, high, carry, carried, limit, offsets, sends_of, tiles, cap, own, final
):
    a_ref, refs = refs[0], refs[1:]
    own_ref, refs = (refs[0], refs[1:]) if own else (None, refs)
    count = len(sends_of)
    sends = (refs[:count], refs[count : 2 * count])
    base_ref, out_ref, kept, store_right, store_left, late = refs[2 * count :]
    stores = (store_right, store_left)
    depth = a_ref.shape[2]
    size = kept.shape[1]
    far = max(offsets)
    panel, step = pl.program_id(0), pl.program_id(1)
    begin = sends_of[0] * SEND if sends_of else 0
    start = low - carry
    wide = size // TW

    @pl.when((panel == 0) & (step == 0))
    def _():
        for side in range(2):
            at = 0
            for ref in sends[side]:
                stores[side][at : at + ref.shape[0]] = ref[...]
                at += ref.shape[0]

    @pl.when(step == 0)
    def _():
        def row_of(slot):
            return place[2 + slot] * depth // TW

        totals = {}
        firsts = {}
        for slot, offset in enumerate(offsets[:high]):
            flags = [b_mask[row_of(slot), place[1] * tiles + j] for j in range(tiles)]
            firsts[offset] = sum(flags[:wide])
            totals[offset] = firsts[offset] + sum(flags[wide:])
        waiting = jnp.int32(0)
        for slot in range(start, high):
            rows = slice((slot - start) * depth, (slot - start + 1) * depth)
            offset = offsets[slot]
            flags = [b_mask[row_of(slot), place[1] * tiles + panel * wide + j] for j in range(wide)]
            if offset == 0:
                for j in range(wide):
                    columns = pl.ds(pl.multiple_of(panel * size + j * TW, TW), TW)
                    kept[rows, j * TW : (j + 1) * TW] = own_ref[:, columns] * flags[j].astype(kept.dtype)
                continue
            total = totals[offset]
            begins = {}
            for sign in (-1, 1):
                begins[sign] = sum(
                    (jnp.maximum(totals[sign * hop], 2 * SEND) for hop in range(1, abs(offset))), jnp.int32(0)
                )
            before = panel * firsts[offset]
            for j, flag in enumerate(flags):
                at = (begins[-1] + before, begins[1] + total - 1 - before)
                columns = slice(j * TW, (j + 1) * TW)
                if offset == far:
                    on_right = at[0] < cap
                    for side, take in ((0, on_right), (1, jnp.logical_not(on_right))):
                        index = jnp.clip(at[side] - begin, 0, stores[side].shape[0] - 1)

                        @pl.when(take)
                        def _():
                            kept[rows, columns] = stores[side][index] * flag.astype(kept.dtype)
                else:
                    side = 0 if offset < 0 else 1
                    valid = flag
                    if slot < low:
                        valid = jnp.where(at[side] >= carried, flag, 0)
                        waiting += valid
                    elif limit is not None:
                        valid = jnp.where(at[side] < limit, flag, 0)
                    index = jnp.clip(at[side] - begin, 0, stores[side].shape[0] - 1)
                    kept[rows, columns] = stores[side][index] * valid.astype(kept.dtype)
                before += flag
        late[0] = waiting

    height = a_ref.shape[1]
    row_count = height // STEPS_OF[final]
    rows = pl.ds(pl.multiple_of(step * row_count, row_count), row_count)
    columns = pl.ds(pl.multiple_of(panel * size, size), size)

    def total_of(from_slot):
        parts = [a_ref[slot, rows, :] for slot in range(from_slot, high)]
        parts = jnp.concatenate(parts, axis=1) if len(parts) > 1 else parts[0]
        product = jnp.dot(parts, kept[(from_slot - start) * depth :, :], preferred_element_type=jnp.float32)
        base = base_ref[...] if low == 0 else base_ref[rows, columns]
        total = base.astype(jnp.float32) + product
        if final:
            out_ref[...] = total.astype(out_ref.dtype)
        else:
            out_ref[rows, columns] = total

    if carry:

        @pl.when(late[0] != 0)
        def _():
            total_of(start)

        @pl.when(late[0] == 0)
        def _():
            total_of(low)

    else:
        total_of(low)


def gather_multiply(
    place, b_mask, a_kept, own, sends, base, *, low, high, carry, carried, limit, offsets, sends_of, cap, width
):
    height, depth = a_kept.shape[1:]
    final = high == len(offsets)
    size = width // 2
    steps = STEPS_OF[final]
    rows = height // steps
    whole = pl.BlockSpec(memory_space=pltpu.VMEM)
    block = pl.BlockSpec((rows, size), lambda p, i, *_: (i, p))
    operands = [place, b_mask, a_kept]
    in_specs = [whole]
    if own is not None:
        operands.append(own)
        in_specs.append(whole)
    for side in range(2):
        arrays = [sends[index][side] for index in sends_of]
        operands += arrays
        in_specs += [whole] * len(arrays)
    store = pltpu.VMEM((max(1, sum(array.shape[0] for array in arrays)), depth, TW), jnp.bfloat16)
    operands.append(base)
    in_specs.append(whole if low else block)
    aliases = {}
    if final:
        out_shape = jax.ShapeDtypeStruct((height, width), jnp.bfloat16)
    else:
        out_shape = pltpu.VMEM((height, width), jnp.float32)
        if low:
            aliases = {len(operands) - 1: 0}
    return pl.pallas_call(
        functools.partial(
            gather_multiply_body, low=low, high=high, carry=carry, carried=carried, limit=limit, offsets=offsets,
            sends_of=sends_of, tiles=width // TW, cap=cap, own=own is not None, final=final,
        ),
        grid_spec=pltpu.PrefetchScalarGridSpec(
            num_scalar_prefetch=2,
            grid=(2, steps),
            in_specs=in_specs,
            out_specs=block if final else whole,
            scratch_shapes=[
                pltpu.VMEM(((high - low + carry) * depth, size), jnp.bfloat16), store, store, pltpu.SMEM((1,), jnp.int32)
            ],
        ),
        out_shape=out_shape,
        input_output_aliases=aliases,
        cost_estimate=pl.CostEstimate(flops=height * size * depth // 16, bytes_accessed=height * size // 16, transcendentals=0),
        compiler_params=pltpu.CompilerParams(vmem_limit_bytes=GATHER_VMEM),
    )(*operands)


def sparse(n, cap, a_tiles, b_tiles, a_mask, b_mask, c_given, plan, *packed):
    ring = ring_of(n)
    right = [(ring[i], ring[(i + 1) % n]) for i in range(n)]
    left = [(t, s) for s, t in right]
    height, width = c_given.shape
    far = n // 2
    panel = width // 2
    tiles = width // TW
    offsets, place = places(n, lax.axis_index("row"), lax.axis_index("col"), height)

    sizes = [SEND] * (cap // SEND) + ([cap % SEND] if cap % SEND else [])
    last = len(sizes)

    def sent_by(count):
        return min(-(-count // SEND), last)

    cut = 1 + 2 * ((far - 1) // 2)
    near, edge = 2 * far - 3, 2 * far - 1
    middle = (sent_by(tiles * (far - 2)) - 1) * SEND
    limit = (last - 1) * SEND
    phases = [
        dict(low=0, high=1, carry=0, carried=0, limit=None, sends_of=()),
        dict(low=1, high=cut, carry=0, carried=0, limit=None, sends_of=(0, sent_by(tiles * (cut // 2)))),
        dict(low=cut, high=near, carry=0, carried=0, limit=middle, sends_of=(2 * (cut // 2), middle // SEND)),
        dict(
            low=near, high=edge, carry=near - cut, carried=middle, limit=limit,
            sends_of=(min(2 * (far - 2), middle // SEND), last - 1),
        ),
        dict(
            low=edge, high=n, carry=edge - near, carried=limit, limit=None,
            sends_of=(min(2 * (far - 1), last - 1), last),
        ),
    ]
    work = collections.defaultdict(list)
    for phase in phases:
        begin, end = phase["sends_of"] or (0, 2)
        phase["sends_of"] = tuple(range(begin, end)) if phase["low"] else ()
        work[min(end + 1, last)].append(phase)

    sends = []
    tied = []
    other = a_kept = total = None
    for index in range(last + 1):
        if index < last:
            if index < 2:
                sources = [packed[index], packed[3 + index]]
            else:
                arrays = []
                for side in range(2):
                    arrays += [packed[3 * side + 2] if index == 2 else sends[index - 3][side], sends[index - 2][side]]
                if tied:
                    *arrays, _ = lax.optimization_barrier((*arrays, tied))
                    tied = []
                sources = choose(plan, arrays, sizes[index])
            sends.append([lax.ppermute(source, "row", pairs) for source, pairs in zip(sources, (right, left))])
        if index == 0:
            other = lax.ppermute(a_tiles, "col", [(0, 1), (1, 0)])
        if index == 1:
            source = pltpu.with_memory_space_constraint(a_tiles, pltpu.HBM)
            a_kept = prepare(place, a_mask, source, other, n)
            tied.append(a_kept)
        for phase in work[index]:
            first = phase["low"] == 0
            total = gather_multiply(
                place, b_mask, a_kept, b_tiles if first else None, sends,
                pltpu.with_memory_space_constraint(c_given, pltpu.HBM) if first else total,
                offsets=tuple(offsets), cap=cap, width=width, **phase,
            )
            tied.append(total)
    return total


def on_device(n, *args):
    b_tiles, b_mask = args[1], args[3]
    *packed, plan = pack(b_mask, b_tiles, n)
    tiles = b_tiles.shape[1] // TW
    most = tiles * (n // 2 - 1) + tiles // 2
    caps = [most - most * saved // 28 for saved in (4,)]
    branches = [functools.partial(sparse, n, cap) for cap in caps]
    branches.append(lambda *operands: dense(n, *operands[:5]))
    which = sum((plan[0] > cap).astype(jnp.int32) for cap in caps)
    return lax.switch(which, branches, *args, plan, *packed)


def solution(mesh):
    return jax.shard_map(
        functools.partial(on_device, mesh.shape["row"]),
        mesh=mesh,
        in_specs=(
            P(("grp", "row"), "col"),
            P(("grp", "row"), "col"),
            P("grp", None),
            P("grp", None),
            P(("grp", "row"), "col"),
        ),
        out_specs=P(("grp", "row"), "col"),
        check_vma=False,
    )
```

```python
import collections
import functools

import jax
import jax.numpy as jnp
from jax import lax
from jax.experimental import pallas as pl
from jax.experimental.pallas import tpu as pltpu
from jax.sharding import PartitionSpec as P

TW = 256
ROWS = 512
LAST_ROWS = 1024
MIB = 1024 * 1024
VMEM = 20 * MIB
SEND = 3
GATHER_VMEM = 16 * MIB
STEPS_OF = {False: 2, True: 2}


def ring_of(n):
    if n == 8:
        return [0, 2, 4, 6, 7, 5, 3, 1]
    return list(range(n))


def prepare_body(place, a_mask, own_ref, other_ref, out_ref, *, depth, n):
    per_half = n // 2
    tiles = own_ref.shape[0] // TW
    for tile in range(tiles):
        rows = slice(tile * TW, (tile + 1) * TW)
        tile_row = place[0] + pl.program_id(0) * tiles + tile
        for away, ref in enumerate((own_ref, other_ref)):
            first = lax.rem(place[1] + away, 2) * per_half
            for index in range(per_half):
                owner = first + index
                flag = a_mask[tile_row, owner * depth // TW].astype(out_ref.dtype)
                out_ref[place[2 + n + owner], rows, :] = ref[rows, index * depth : (index + 1) * depth] * flag


def prepare(place, a_mask, own, other, n):
    height, half = own.shape
    depth = 2 * half // n
    return pl.pallas_call(
        functools.partial(prepare_body, depth=depth, n=n),
        grid_spec=pltpu.PrefetchScalarGridSpec(
            num_scalar_prefetch=2,
            grid=(height // ROWS,),
            in_specs=[pl.BlockSpec((ROWS, half), lambda i, *_: (i, 0))] * 2,
            out_specs=pl.BlockSpec((n, ROWS, depth), lambda i, *_: (0, i, 0)),
        ),
        out_shape=pltpu.VMEM((n, height, depth), jnp.bfloat16),
        cost_estimate=pl.CostEstimate(flops=0, bytes_accessed=height * half // 16, transcendentals=0),
        compiler_params=pltpu.CompilerParams(vmem_limit_bytes=VMEM),
    )(place, a_mask, own, other)


def multiply_body(place, b_mask, *refs, layout, low, high, first, chained):
    left, refs = refs[: high - low], refs[high - low :]
    blocks = refs[: len(layout)]
    base_ref = refs[len(layout)]
    out_ref, kept = refs[len(layout) + 1 + chained :]
    depth = blocks[0].shape[0]

    @pl.when(pl.program_id(0) == 0)
    def _():
        for ref, (slot, shift) in zip(blocks, layout):
            tile_k = place[2 + slot] * depth // TW
            for j in range(ref.shape[1] // TW):
                at = shift + j * TW
                flag = b_mask[tile_k, place[1] * 8 + (first + at) // TW].astype(kept.dtype)
                block = ref[:, j * TW : (j + 1) * TW]
                kept[(slot - low) * depth : (slot - low + 1) * depth, at : at + TW] = block * flag

    left = [ref[0] for ref in left]
    left = jnp.concatenate(left, axis=1) if len(left) > 1 else left[0]
    product = jnp.dot(left, kept[...], preferred_element_type=jnp.float32)
    out_ref[...] = (base_ref[...].astype(jnp.float32) + product).astype(out_ref.dtype)


def multiply(place, b_mask, a_kept, arrived, base, base_column, out, *, low, high, first, size, wide, width):
    height = a_kept.shape[1]
    depth = arrived[0][2].shape[0]
    rows = LAST_ROWS if high - low == 1 else ROWS
    operands = [place, b_mask] + [a_kept] * (high - low)
    whole = pl.BlockSpec(memory_space=pltpu.VMEM)
    in_specs = [
        pl.BlockSpec((1, rows, depth), functools.partial(lambda slot, i, *_: (slot, i, 0), slot)) for slot in range(low, high)
    ]
    for _, _, array in arrived:
        operands.append(array)
        if array.shape[1] == width:
            in_specs.append(pl.BlockSpec((depth, size), lambda i, *_: (0, first // size)))
        else:
            in_specs.append(whole)
    operands.append(base)
    in_specs.append(pl.BlockSpec((rows, size), lambda i, *_: (i, base_column // size)))
    if wide:
        out_shape = pltpu.VMEM((height, size), jnp.float32)
        out_spec = pl.BlockSpec((rows, size), lambda i, *_: (i, 0))
    else:
        out_shape = jax.ShapeDtypeStruct((height, width), jnp.bfloat16)
        out_spec = pl.BlockSpec((rows, size), lambda i, *_: (i, first // size))
    aliases = {}
    if out is not None:
        aliases = {len(operands): 0}
        operands.append(pltpu.with_memory_space_constraint(out, pltpu.HBM))
        in_specs.append(pl.BlockSpec(memory_space=pl.ANY))
    extent = (high - low) * depth
    return pl.pallas_call(
        functools.partial(
            multiply_body,
            layout=tuple((slot, shift) for slot, shift, _ in arrived),
            low=low,
            high=high,
            first=first,
            chained=out is not None,
        ),
        grid_spec=pltpu.PrefetchScalarGridSpec(
            num_scalar_prefetch=2,
            grid=(height // rows,),
            in_specs=in_specs,
            out_specs=out_spec,
            scratch_shapes=[pltpu.VMEM((extent, size), jnp.bfloat16)],
        ),
        out_shape=out_shape,
        input_output_aliases=aliases,
        cost_estimate=pl.CostEstimate(
            flops=height * size * extent // 16, bytes_accessed=height * size // 16, transcendentals=0
        ),
        compiler_params=pltpu.CompilerParams(vmem_limit_bytes=VMEM),
    )(*operands)


def places(n, row, col, height):
    ring = ring_of(n)
    far = n // 2
    offsets = [0] + [sign * hop for hop in range(1, far) for sign in (-1, 1)] + [far]
    table = []
    for r in range(n):
        owners = [ring[(ring.index(r) + o) % n] for o in offsets]
        table.append(owners + [owners.index(owner) for owner in range(n)])
    table = lax.dynamic_index_in_dim(jnp.array(table, jnp.int32), row, 0, keepdims=False)
    return offsets, jnp.concatenate([jnp.stack([row * (height // TW), col]).astype(jnp.int32), table])


def dense(n, a_tiles, b_tiles, a_mask, b_mask, c_given):
    ring = ring_of(n)
    right = [(ring[i], ring[(i + 1) % n]) for i in range(n)]
    left = [(t, s) for s, t in right]
    row = lax.axis_index("row")
    col = lax.axis_index("col")
    height, width = c_given.shape
    far = n // 2
    panel = width // 2

    offsets, place = places(n, row, col, height)

    rounds = [(p, hop, 0, panel) for hop in range(1, far) for p in range(2)]
    rounds += [(0, far, 0, panel), (1, far, 0, panel)]
    work = collections.defaultdict(list)
    last = len(rounds)
    work[last - 4] = [(0, 0, n - 3, 0, panel)]
    work[last - 3] = [(1, 0, n - 3, 0, panel)]
    work[last - 2] = [(0, n - 3, n - 1, 0, panel)]
    work[last] = [(1, n - 3, n - 1, 0, panel), (0, n - 1, n, 0, panel), (1, n - 1, n, 0, panel)]

    blocks = [{0: b_tiles} for _ in range(2)]
    other = a_kept = out = None
    wide = {}
    tied = []
    for index in range(last + 1):
        if index < last:
            p, hop, start, stop = rounds[index]
            sources = []
            for sign in (-1, 1):
                if hop == 1:
                    source = b_tiles[:, p * panel : (p + 1) * panel]
                else:
                    source = blocks[p][sign * (hop - 1)]
                if hop == far:
                    middle = (start + stop) // 2
                    source = source[:, start:middle] if sign < 0 else source[:, middle:stop]
                sources.append(source)
            if tied:
                *sources, _ = lax.optimization_barrier((*sources, tied))
            tied = []
            for sign, pairs, source in zip((-1, 1), (right, left), sources):
                key = (sign * hop, start) if hop == far else sign * hop
                blocks[p][key] = lax.ppermute(source, "row", pairs)
        if index == 0:
            other = lax.ppermute(a_tiles, "col", [(0, 1), (1, 0)])
        if index == 1:
            source = pltpu.with_memory_space_constraint(a_tiles, pltpu.HBM)
            a_kept = prepare(place, a_mask, source, other, n)
            tied.append(a_kept)
        for p, low, high, start, stop in work[index]:
            arrived = []
            for slot in range(low, high):
                if offsets[slot] == far:
                    arrived.append((slot, 0, blocks[p][-far, start]))
                    arrived.append((slot, (stop - start) // 2, blocks[p][far, start]))
                else:
                    arrived.append((slot, 0, blocks[p][offsets[slot]]))
            done = high == n
            if low:
                base, base_column = wide[p], start
            else:
                base, base_column = pltpu.with_memory_space_constraint(c_given, pltpu.HBM), p * panel + start
            result = multiply(
                place, b_mask, a_kept, arrived, base, base_column, out if done else None,
                low=low, high=high, first=p * panel + start, size=stop - start, wide=not done, width=width,
            )
            tied.append(result)
            if done:
                out = result
            else:
                wide[p] = result
    return out


def pack_body(b_mask, b_ref, *refs, n, tiles, head):
    depth = b_ref.shape[0]
    arrived = refs[-1]
    mine = lax.axis_index("row") * depth // TW
    half = lax.axis_index("col") * tiles
    flags = [b_mask[mine, half + j] for j in range(tiles)]
    total = sum(flags)
    end = jnp.maximum(total, 2 * SEND)

    def put(ref, low, j, at):
        @pl.when((at >= low) & (at < low + SEND))
        def _():
            pltpu.make_async_copy(b_ref.at[:, j * TW : (j + 1) * TW], ref.at[at - low], arrived).start()

    before = jnp.int32(0)
    for j in range(tiles):
        dropped = total + j - before
        places = (jnp.where(flags[j] != 0, before, dropped), jnp.where(flags[j] != 0, total - 1 - before, dropped))
        for side, at in enumerate(places):
            if head:
                put(refs[side], 0, j, at)
            else:
                put(refs[2 * side], SEND, j, at)
                put(refs[2 * side + 1], end - SEND, j, at)
        before += flags[j]

    if head:
        plan = refs[2]
        ring = ring_of(n)
        far = n // 2
        need = jnp.int32(0)
        for c in range(2):
            kept = []
            for owner in ring:
                count = jnp.int32(0)
                for j in range(tiles):
                    count += b_mask[owner * depth // TW, c * tiles + j]
                kept.append(count)
            span = [jnp.maximum(count, 2 * SEND) for count in kept]
            for q in range(n):
                right = sum(span[(q - hop) % n] for hop in range(1, far))
                left = sum(span[(q + hop) % n] for hop in range(1, far))
                both = lax.shift_right_logical(right + left + kept[(q + far) % n] + 1, 1)
                need = jnp.maximum(need, jnp.maximum(jnp.maximum(right, left), both))
        plan[0] = need
        plan[1] = 3 * SEND - end
    for ref in refs[: 2 if head else 4]:
        pltpu.make_async_copy(ref, ref, arrived).wait()


def pack(b_mask, b_tiles, n, head):
    depth, width = b_tiles.shape
    whole = pl.BlockSpec(memory_space=pltpu.VMEM)
    count = 2 if head else 4
    out_shape = [pltpu.VMEM((SEND, depth, TW), jnp.bfloat16)] * count
    out_specs = [whole] * count
    if head:
        out_shape.append(jax.ShapeDtypeStruct((2,), jnp.int32))
        out_specs.append(pl.BlockSpec(memory_space=pltpu.SMEM))
    return pl.pallas_call(
        functools.partial(pack_body, n=n, tiles=width // TW, head=head),
        grid_spec=pltpu.PrefetchScalarGridSpec(
            num_scalar_prefetch=1,
            grid=(1,),
            in_specs=[pl.BlockSpec(memory_space=pl.ANY)],
            out_specs=out_specs,
            scratch_shapes=[pltpu.SemaphoreType.DMA],
        ),
        out_shape=out_shape,
        cost_estimate=pl.CostEstimate(flops=0, bytes_accessed=1024, transcendentals=0),
        compiler_params=pltpu.CompilerParams(vmem_limit_bytes=VMEM),
    )(b_mask, pltpu.with_memory_space_constraint(b_tiles, pltpu.HBM))


def choose_body(plan, *refs, count):
    for before, last, out in (refs[0:2] + refs[4:5], refs[2:4] + refs[5:6]):
        for start in range(1, SEND + 1):

            @pl.when(plan[1] == start)
            def _():
                for i in range(count):
                    at = start + i
                    out[i] = before[at] if at < SEND else last[at - SEND]


def choose(plan, arrays, count):
    shape = (count,) + arrays[0].shape[1:]
    whole = pl.BlockSpec(memory_space=pltpu.VMEM)
    return pl.pallas_call(
        functools.partial(choose_body, count=count),
        grid_spec=pltpu.PrefetchScalarGridSpec(
            num_scalar_prefetch=1, grid=(1,), in_specs=[whole] * 4, out_specs=[whole] * 2
        ),
        out_shape=[pltpu.VMEM(shape, jnp.bfloat16)] * 2,
        cost_estimate=pl.CostEstimate(flops=0, bytes_accessed=1024, transcendentals=0),
        compiler_params=pltpu.CompilerParams(vmem_limit_bytes=VMEM),
    )(plan, *arrays)


def gather_multiply_body(
    place, b_mask, *refs, low, high, carry, carried, limit, offsets, sends_of, tiles, cap, own, final
):
    a_ref, refs = refs[0], refs[1:]
    own_ref, refs = (refs[0], refs[1:]) if own else (None, refs)
    count = len(sends_of)
    sends = (refs[:count], refs[count : 2 * count])
    base_ref, out_ref, kept, store_right, store_left, late = refs[2 * count :]
    stores = (store_right, store_left)
    depth = a_ref.shape[2]
    size = kept.shape[1]
    far = max(offsets)
    panel, step = pl.program_id(0), pl.program_id(1)
    begin = sends_of[0] * SEND if sends_of else 0
    start = low - carry
    wide = size // TW

    @pl.when((panel == 0) & (step == 0))
    def _():
        for side in range(2):
            at = 0
            for ref in sends[side]:
                stores[side][at : at + ref.shape[0]] = ref[...]
                at += ref.shape[0]

    @pl.when(step == 0)
    def _():
        def row_of(slot):
            return place[2 + slot] * depth // TW

        totals = {}
        firsts = {}
        for slot, offset in enumerate(offsets[:high]):
            flags = [b_mask[row_of(slot), place[1] * tiles + j] for j in range(tiles)]
            firsts[offset] = sum(flags[:wide])
            totals[offset] = firsts[offset] + sum(flags[wide:])
        waiting = jnp.int32(0)
        leftover = []
        for slot in range(start, high):
            rows = slice((slot - start) * depth, (slot - start + 1) * depth)
            offset = offsets[slot]
            flags = [b_mask[row_of(slot), place[1] * tiles + panel * wide + j] for j in range(wide)]
            if offset == 0:
                for j in range(wide):
                    columns = pl.ds(pl.multiple_of(panel * size + j * TW, TW), TW)
                    kept[rows, j * TW : (j + 1) * TW] = own_ref[:, columns] * flags[j].astype(kept.dtype)
                continue
            total = totals[offset]
            begins = {}
            for sign in (-1, 1):
                begins[sign] = sum(
                    (jnp.maximum(totals[sign * hop], 2 * SEND) for hop in range(1, abs(offset))), jnp.int32(0)
                )
            before = panel * firsts[offset]
            for j, flag in enumerate(flags):
                at = (begins[-1] + before, begins[1] + total - 1 - before)
                columns = slice(j * TW, (j + 1) * TW)
                if offset == far:
                    on_right = at[0] < cap
                    for side, take in ((0, on_right), (1, jnp.logical_not(on_right))):
                        index = jnp.clip(at[side] - begin, 0, stores[side].shape[0] - 1)

                        @pl.when(take)
                        def _():
                            kept[rows, columns] = stores[side][index] * flag.astype(kept.dtype)
                else:
                    side = 0 if offset < 0 else 1
                    valid = flag
                    index = jnp.clip(at[side] - begin, 0, stores[side].shape[0] - 1)
                    if slot < low:
                        valid = jnp.where(at[side] >= carried, flag, 0)
                        waiting += valid
                        leftover.append((rows, columns, side, index, valid))
                    else:
                        if limit is not None:
                            valid = jnp.where(at[side] < limit, flag, 0)
                        kept[rows, columns] = stores[side][index] * valid.astype(kept.dtype)
                before += flag
        late[0] = waiting
        if carry:

            @pl.when(waiting != 0)
            def _():
                for rows, columns, side, index, valid in leftover:
                    kept[rows, columns] = stores[side][index] * valid.astype(kept.dtype)


    height = a_ref.shape[1]
    row_count = height // STEPS_OF[final]
    rows = pl.ds(pl.multiple_of(step * row_count, row_count), row_count)
    columns = pl.ds(pl.multiple_of(panel * size, size), size)

    def total_of(from_slot):
        parts = [a_ref[slot, rows, :] for slot in range(from_slot, high)]
        parts = jnp.concatenate(parts, axis=1) if len(parts) > 1 else parts[0]
        product = jnp.dot(parts, kept[(from_slot - start) * depth :, :], preferred_element_type=jnp.float32)
        base = base_ref[...] if low == 0 else base_ref[rows, columns]
        total = base.astype(jnp.float32) + product
        if final:
            out_ref[...] = total.astype(out_ref.dtype)
        else:
            out_ref[rows, columns] = total

    if carry:

        @pl.when(late[0] != 0)
        def _():
            total_of(start)

        @pl.when(late[0] == 0)
        def _():
            total_of(low)

    else:
        total_of(low)


def gather_multiply(
    place, b_mask, a_kept, own, sends, base, *, low, high, carry, carried, limit, offsets, sends_of, cap, width
):
    height, depth = a_kept.shape[1:]
    final = high == len(offsets)
    size = width // 2
    steps = STEPS_OF[final]
    rows = height // steps
    whole = pl.BlockSpec(memory_space=pltpu.VMEM)
    block = pl.BlockSpec((rows, size), lambda p, i, *_: (i, p))
    operands = [place, b_mask, a_kept]
    in_specs = [whole]
    if own is not None:
        operands.append(own)
        in_specs.append(whole)
    for side in range(2):
        arrays = [sends[index][side] for index in sends_of]
        operands += arrays
        in_specs += [whole] * len(arrays)
    store = pltpu.VMEM((max(1, sum(array.shape[0] for array in arrays)), depth, TW), jnp.bfloat16)
    operands.append(base)
    in_specs.append(whole if low else block)
    aliases = {}
    if final:
        out_shape = jax.ShapeDtypeStruct((height, width), jnp.bfloat16)
    else:
        out_shape = pltpu.VMEM((height, width), jnp.float32)
        if low:
            aliases = {len(operands) - 1: 0}
    return pl.pallas_call(
        functools.partial(
            gather_multiply_body, low=low, high=high, carry=carry, carried=carried, limit=limit, offsets=offsets,
            sends_of=sends_of, tiles=width // TW, cap=cap, own=own is not None, final=final,
        ),
        grid_spec=pltpu.PrefetchScalarGridSpec(
            num_scalar_prefetch=2,
            grid=(2, steps),
            in_specs=in_specs,
            out_specs=block if final else whole,
            scratch_shapes=[
                pltpu.VMEM(((high - low + carry) * depth, size), jnp.bfloat16), store, store, pltpu.SMEM((1,), jnp.int32)
            ],
        ),
        out_shape=out_shape,
        input_output_aliases=aliases,
        cost_estimate=pl.CostEstimate(flops=height * size * depth // 16, bytes_accessed=height * size // 16, transcendentals=0),
        compiler_params=pltpu.CompilerParams(vmem_limit_bytes=GATHER_VMEM),
    )(*operands)


def sparse(n, cap, a_tiles, b_tiles, a_mask, b_mask, c_given, plan, *heads):
    ring = ring_of(n)
    right = [(ring[i], ring[(i + 1) % n]) for i in range(n)]
    left = [(t, s) for s, t in right]
    height, width = c_given.shape
    far = n // 2
    panel = width // 2
    tiles = width // TW
    offsets, place = places(n, lax.axis_index("row"), lax.axis_index("col"), height)

    sizes = [SEND] * (cap // SEND) + ([cap % SEND] if cap % SEND else [])
    last = len(sizes)

    def sent_by(count):
        return min(-(-count // SEND), last)

    cut = 1 + 2 * ((far - 1) // 2)
    near, edge = 2 * far - 3, 2 * far - 1
    middle = (sent_by(tiles * (far - 2)) - 1) * SEND
    limit = (cap - 2) // SEND * SEND
    phases = [
        dict(low=0, high=1, carry=0, carried=0, limit=None, sends_of=()),
        dict(low=1, high=cut, carry=0, carried=0, limit=None, sends_of=(0, sent_by(tiles * (cut // 2)))),
        dict(low=cut, high=near, carry=0, carried=0, limit=middle, sends_of=(2 * (cut // 2), middle // SEND)),
        dict(
            low=near, high=edge, carry=near - cut, carried=middle, limit=limit,
            sends_of=(min(2 * (far - 2), middle // SEND), limit // SEND),
        ),
        dict(
            low=edge, high=n, carry=edge - near, carried=limit, limit=None,
            sends_of=(min(2 * (far - 1), limit // SEND), last),
        ),
    ]
    work = collections.defaultdict(list)
    for phase in phases:
        begin, end = phase["sends_of"] or (0, 2)
        phase["sends_of"] = tuple(range(begin, end)) if phase["low"] else ()
        work[min(end + 1, last)].append(phase)

    sends = []
    tied = []
    other = a_kept = total = None
    for index in range(last + 1):
        if index < last:
            if index == 0:
                sources = heads
            elif index == 1:
                packed = pack(b_mask, b_tiles, n, False)
                sources = packed[::2]
            else:
                arrays = []
                for side in range(2):
                    arrays += [packed[2 * side + 1] if index == 2 else sends[index - 3][side], sends[index - 2][side]]
                if tied:
                    *arrays, _ = lax.optimization_barrier((*arrays, tied))
                    tied = []
                sources = choose(plan, arrays, sizes[index])
            sends.append([lax.ppermute(source, "row", pairs) for source, pairs in zip(sources, (right, left))])
        if index == 0:
            other = lax.ppermute(a_tiles, "col", [(0, 1), (1, 0)])
        if index == 1:
            source = pltpu.with_memory_space_constraint(a_tiles, pltpu.HBM)
            a_kept = prepare(place, a_mask, source, other, n)
            tied.append(a_kept)
        for phase in work[index]:
            first = phase["low"] == 0
            total = gather_multiply(
                place, b_mask, a_kept, b_tiles if first else None, sends,
                pltpu.with_memory_space_constraint(c_given, pltpu.HBM) if first else total,
                offsets=tuple(offsets), cap=cap, width=width, **phase,
            )
            tied.append(total)
    return total


def on_device(n, *args):
    b_tiles, b_mask = args[1], args[3]
    *heads, plan = pack(b_mask, b_tiles, n, True)
    tiles = b_tiles.shape[1] // TW
    most = tiles * (n // 2 - 1) + tiles // 2
    caps = [most - most * saved // 28 for saved in (4, 3)]
    branches = [functools.partial(sparse, n, cap) for cap in caps]
    branches.append(lambda *operands: dense(n, *operands[:5]))
    which = sum((plan[0] > cap).astype(jnp.int32) for cap in caps)
    return lax.switch(which, branches, *args, plan, *heads)


def solution(mesh):
    return jax.shard_map(
        functools.partial(on_device, mesh.shape["row"]),
        mesh=mesh,
        in_specs=(
            P(("grp", "row"), "col"),
            P(("grp", "row"), "col"),
            P("grp", None),
            P("grp", None),
            P(("grp", "row"), "col"),
        ),
        out_specs=P(("grp", "row"), "col"),
        check_vma=False,
    )
```

```python
import collections
import functools

import jax
import jax.numpy as jnp
from jax import lax
from jax.experimental import pallas as pl
from jax.experimental.pallas import tpu as pltpu
from jax.sharding import PartitionSpec as P

TW = 256
ROWS = 512
LAST_ROWS = 1024
MIB = 1024 * 1024
VMEM = 20 * MIB
SEND = 3
GATHER_VMEM = 16 * MIB
STEPS_OF = {False: 2, True: 2}
PIECE = (256, 512)


def ring_of(n):
    if n == 8:
        return [0, 2, 4, 6, 7, 5, 3, 1]
    return list(range(n))


def prepare_body(place, a_mask, own_ref, other_ref, out_ref, *, depth, n):
    per_half = n // 2
    tiles = own_ref.shape[0] // TW
    for tile in range(tiles):
        rows = slice(tile * TW, (tile + 1) * TW)
        tile_row = place[0] + pl.program_id(0) * tiles + tile
        for away, ref in enumerate((own_ref, other_ref)):
            first = lax.rem(place[1] + away, 2) * per_half
            for index in range(per_half):
                owner = first + index
                flag = a_mask[tile_row, owner * depth // TW].astype(out_ref.dtype)
                out_ref[place[2 + n + owner], rows, :] = ref[rows, index * depth : (index + 1) * depth] * flag


def prepare(place, a_mask, own, other, n):
    height, half = own.shape
    depth = 2 * half // n
    return pl.pallas_call(
        functools.partial(prepare_body, depth=depth, n=n),
        grid_spec=pltpu.PrefetchScalarGridSpec(
            num_scalar_prefetch=2,
            grid=(height // ROWS,),
            in_specs=[pl.BlockSpec((ROWS, half), lambda i, *_: (i, 0))] * 2,
            out_specs=pl.BlockSpec((n, ROWS, depth), lambda i, *_: (0, i, 0)),
        ),
        out_shape=pltpu.VMEM((n, height, depth), jnp.bfloat16),
        cost_estimate=pl.CostEstimate(flops=0, bytes_accessed=height * half // 16, transcendentals=0),
        compiler_params=pltpu.CompilerParams(vmem_limit_bytes=VMEM),
    )(place, a_mask, own, other)


def multiply_body(place, b_mask, *refs, layout, low, high, first, chained):
    left, refs = refs[: high - low], refs[high - low :]
    blocks = refs[: len(layout)]
    base_ref = refs[len(layout)]
    out_ref, kept = refs[len(layout) + 1 + chained :]
    depth = blocks[0].shape[0]

    @pl.when(pl.program_id(0) == 0)
    def _():
        for ref, (slot, shift) in zip(blocks, layout):
            tile_k = place[2 + slot] * depth // TW
            for j in range(ref.shape[1] // TW):
                at = shift + j * TW
                flag = b_mask[tile_k, place[1] * 8 + (first + at) // TW].astype(kept.dtype)
                block = ref[:, j * TW : (j + 1) * TW]
                kept[(slot - low) * depth : (slot - low + 1) * depth, at : at + TW] = block * flag

    left = [ref[0] for ref in left]
    left = jnp.concatenate(left, axis=1) if len(left) > 1 else left[0]
    product = jnp.dot(left, kept[...], preferred_element_type=jnp.float32)
    out_ref[...] = (base_ref[...].astype(jnp.float32) + product).astype(out_ref.dtype)


def multiply(place, b_mask, a_kept, arrived, base, base_column, out, *, low, high, first, size, wide, width):
    height = a_kept.shape[1]
    depth = arrived[0][2].shape[0]
    rows = LAST_ROWS if high - low == 1 else ROWS
    operands = [place, b_mask] + [a_kept] * (high - low)
    whole = pl.BlockSpec(memory_space=pltpu.VMEM)
    in_specs = [
        pl.BlockSpec((1, rows, depth), functools.partial(lambda slot, i, *_: (slot, i, 0), slot)) for slot in range(low, high)
    ]
    for _, _, array in arrived:
        operands.append(array)
        if array.shape[1] == width:
            in_specs.append(pl.BlockSpec((depth, size), lambda i, *_: (0, first // size)))
        else:
            in_specs.append(whole)
    operands.append(base)
    in_specs.append(pl.BlockSpec((rows, size), lambda i, *_: (i, base_column // size)))
    if wide:
        out_shape = pltpu.VMEM((height, size), jnp.float32)
        out_spec = pl.BlockSpec((rows, size), lambda i, *_: (i, 0))
    else:
        out_shape = jax.ShapeDtypeStruct((height, width), jnp.bfloat16)
        out_spec = pl.BlockSpec((rows, size), lambda i, *_: (i, first // size))
    aliases = {}
    if out is not None:
        aliases = {len(operands): 0}
        operands.append(pltpu.with_memory_space_constraint(out, pltpu.HBM))
        in_specs.append(pl.BlockSpec(memory_space=pl.ANY))
    extent = (high - low) * depth
    return pl.pallas_call(
        functools.partial(
            multiply_body,
            layout=tuple((slot, shift) for slot, shift, _ in arrived),
            low=low,
            high=high,
            first=first,
            chained=out is not None,
        ),
        grid_spec=pltpu.PrefetchScalarGridSpec(
            num_scalar_prefetch=2,
            grid=(height // rows,),
            in_specs=in_specs,
            out_specs=out_spec,
            scratch_shapes=[pltpu.VMEM((extent, size), jnp.bfloat16)],
        ),
        out_shape=out_shape,
        input_output_aliases=aliases,
        cost_estimate=pl.CostEstimate(
            flops=height * size * extent // 16, bytes_accessed=height * size // 16, transcendentals=0
        ),
        compiler_params=pltpu.CompilerParams(vmem_limit_bytes=VMEM),
    )(*operands)


def places(n, row, col, height):
    ring = ring_of(n)
    far = n // 2
    offsets = [0] + [sign * hop for hop in range(1, far) for sign in (-1, 1)] + [far]
    table = []
    for r in range(n):
        owners = [ring[(ring.index(r) + o) % n] for o in offsets]
        table.append(owners + [owners.index(owner) for owner in range(n)])
    table = lax.dynamic_index_in_dim(jnp.array(table, jnp.int32), row, 0, keepdims=False)
    return offsets, jnp.concatenate([jnp.stack([row * (height // TW), col]).astype(jnp.int32), table])


def dense(n, a_tiles, b_tiles, a_mask, b_mask, c_given):
    ring = ring_of(n)
    right = [(ring[i], ring[(i + 1) % n]) for i in range(n)]
    left = [(t, s) for s, t in right]
    row = lax.axis_index("row")
    col = lax.axis_index("col")
    height, width = c_given.shape
    far = n // 2
    panel = width // 2

    offsets, place = places(n, row, col, height)

    rounds = [(p, hop, 0, panel) for hop in range(1, far) for p in range(2)]
    rounds += [(0, far, 0, panel), (1, far, 0, panel)]
    work = collections.defaultdict(list)
    last = len(rounds)
    work[last - 4] = [(0, 0, n - 3, 0, panel)]
    work[last - 3] = [(1, 0, n - 3, 0, panel)]
    work[last - 2] = [(0, n - 3, n - 1, 0, panel)]
    work[last] = [(1, n - 3, n - 1, 0, panel), (0, n - 1, n, 0, panel), (1, n - 1, n, 0, panel)]

    blocks = [{0: b_tiles} for _ in range(2)]
    other = a_kept = out = None
    wide = {}
    tied = []
    for index in range(last + 1):
        if index < last:
            p, hop, start, stop = rounds[index]
            sources = []
            for sign in (-1, 1):
                if hop == 1:
                    source = b_tiles[:, p * panel : (p + 1) * panel]
                else:
                    source = blocks[p][sign * (hop - 1)]
                if hop == far:
                    middle = (start + stop) // 2
                    source = source[:, start:middle] if sign < 0 else source[:, middle:stop]
                sources.append(source)
            if tied:
                *sources, _ = lax.optimization_barrier((*sources, tied))
            tied = []
            for sign, pairs, source in zip((-1, 1), (right, left), sources):
                key = (sign * hop, start) if hop == far else sign * hop
                blocks[p][key] = lax.ppermute(source, "row", pairs)
        if index == 0:
            other = lax.ppermute(a_tiles, "col", [(0, 1), (1, 0)])
        if index == 1:
            source = pltpu.with_memory_space_constraint(a_tiles, pltpu.HBM)
            a_kept = prepare(place, a_mask, source, other, n)
            tied.append(a_kept)
        for p, low, high, start, stop in work[index]:
            arrived = []
            for slot in range(low, high):
                if offsets[slot] == far:
                    arrived.append((slot, 0, blocks[p][-far, start]))
                    arrived.append((slot, (stop - start) // 2, blocks[p][far, start]))
                else:
                    arrived.append((slot, 0, blocks[p][offsets[slot]]))
            done = high == n
            if low:
                base, base_column = wide[p], start
            else:
                base, base_column = pltpu.with_memory_space_constraint(c_given, pltpu.HBM), p * panel + start
            result = multiply(
                place, b_mask, a_kept, arrived, base, base_column, out if done else None,
                low=low, high=high, first=p * panel + start, size=stop - start, wide=not done, width=width,
            )
            tied.append(result)
            if done:
                out = result
            else:
                wide[p] = result
    return out


def pack_body(b_mask, b_ref, *refs, n, tiles, head):
    depth = b_ref.shape[0]
    arrived = refs[-1]
    mine = lax.axis_index("row") * depth // TW
    half = lax.axis_index("col") * tiles
    flags = [b_mask[mine, half + j] for j in range(tiles)]
    total = sum(flags)
    end = jnp.maximum(total, 2 * SEND)

    def put(ref, low, j, at):
        @pl.when((at >= low) & (at < low + SEND))
        def _():
            pltpu.make_async_copy(b_ref.at[:, j * TW : (j + 1) * TW], ref.at[at - low], arrived).start()

    before = jnp.int32(0)
    for j in range(tiles):
        dropped = total + j - before
        places = (jnp.where(flags[j] != 0, before, dropped), jnp.where(flags[j] != 0, total - 1 - before, dropped))
        for side, at in enumerate(places):
            if head:
                put(refs[side], 0, j, at)
            else:
                put(refs[2 * side], SEND, j, at)
                put(refs[2 * side + 1], end - SEND, j, at)
        before += flags[j]

    if head:
        plan = refs[2]
        ring = ring_of(n)
        far = n // 2
        need = jnp.int32(0)
        for c in range(2):
            kept = []
            for owner in ring:
                count = jnp.int32(0)
                for j in range(tiles):
                    count += b_mask[owner * depth // TW, c * tiles + j]
                kept.append(count)
            span = [jnp.maximum(count, 2 * SEND) for count in kept]
            for q in range(n):
                right = sum(span[(q - hop) % n] for hop in range(1, far))
                left = sum(span[(q + hop) % n] for hop in range(1, far))
                both = lax.shift_right_logical(right + left + kept[(q + far) % n] + 1, 1)
                need = jnp.maximum(need, jnp.maximum(jnp.maximum(right, left), both))
        plan[0] = need
        plan[1] = 3 * SEND - end
    for ref in refs[: 2 if head else 4]:
        pltpu.make_async_copy(ref, ref, arrived).wait()


def pack(b_mask, b_tiles, n, head):
    depth, width = b_tiles.shape
    whole = pl.BlockSpec(memory_space=pltpu.VMEM)
    count = 2 if head else 4
    out_shape = [pltpu.VMEM((SEND, depth, TW), jnp.bfloat16)] * count
    out_specs = [whole] * count
    if head:
        out_shape.append(jax.ShapeDtypeStruct((2,), jnp.int32))
        out_specs.append(pl.BlockSpec(memory_space=pltpu.SMEM))
    return pl.pallas_call(
        functools.partial(pack_body, n=n, tiles=width // TW, head=head),
        grid_spec=pltpu.PrefetchScalarGridSpec(
            num_scalar_prefetch=1,
            grid=(1,),
            in_specs=[pl.BlockSpec(memory_space=pl.ANY)],
            out_specs=out_specs,
            scratch_shapes=[pltpu.SemaphoreType.DMA],
        ),
        out_shape=out_shape,
        cost_estimate=pl.CostEstimate(flops=0, bytes_accessed=1024, transcendentals=0),
        compiler_params=pltpu.CompilerParams(vmem_limit_bytes=VMEM),
    )(b_mask, pltpu.with_memory_space_constraint(b_tiles, pltpu.HBM))


def choose_body(plan, *refs, count):
    for before, last, out in (refs[0:2] + refs[4:5], refs[2:4] + refs[5:6]):
        for start in range(1, SEND + 1):

            @pl.when(plan[1] == start)
            def _():
                for i in range(count):
                    at = start + i
                    out[i] = before[at] if at < SEND else last[at - SEND]


def choose(plan, arrays, count):
    shape = (count,) + arrays[0].shape[1:]
    whole = pl.BlockSpec(memory_space=pltpu.VMEM)
    return pl.pallas_call(
        functools.partial(choose_body, count=count),
        grid_spec=pltpu.PrefetchScalarGridSpec(
            num_scalar_prefetch=1, grid=(1,), in_specs=[whole] * 4, out_specs=[whole] * 2
        ),
        out_shape=[pltpu.VMEM(shape, jnp.bfloat16)] * 2,
        cost_estimate=pl.CostEstimate(flops=0, bytes_accessed=1024, transcendentals=0),
        compiler_params=pltpu.CompilerParams(vmem_limit_bytes=VMEM),
    )(plan, *arrays)


def gather_multiply_body(
    place, b_mask, *refs, low, high, carry, carried, limit, offsets, sends_of, tiles, cap, own, final
):
    a_ref, refs = refs[0], refs[1:]
    own_ref, refs = (refs[0], refs[1:]) if own else (None, refs)
    count = len(sends_of)
    sends = (refs[:count], refs[count : 2 * count])
    base_ref, out_ref, kept, store_right, store_left, late, *rest = refs[2 * count :]
    done, written = rest if final else (None, None)
    stores = (store_right, store_left)
    depth = a_ref.shape[2]
    size = kept.shape[1]
    far = max(offsets)
    panel, step = pl.program_id(0), pl.program_id(1)
    begin = sends_of[0] * SEND if sends_of else 0
    start = low - carry
    wide = size // TW

    @pl.when((panel == 0) & (step == 0))
    def _():
        for side in range(2):
            at = 0
            for ref in sends[side]:
                stores[side][at : at + ref.shape[0]] = ref[...]
                at += ref.shape[0]

    @pl.when(step == 0)
    def _():
        def row_of(slot):
            return place[2 + slot] * depth // TW

        totals = {}
        firsts = {}
        for slot, offset in enumerate(offsets[:high]):
            flags = [b_mask[row_of(slot), place[1] * tiles + j] for j in range(tiles)]
            firsts[offset] = sum(flags[:wide])
            totals[offset] = firsts[offset] + sum(flags[wide:])
        waiting = jnp.int32(0)
        leftover = []
        for slot in range(start, high):
            rows = slice((slot - start) * depth, (slot - start + 1) * depth)
            offset = offsets[slot]
            flags = [b_mask[row_of(slot), place[1] * tiles + panel * wide + j] for j in range(wide)]
            if offset == 0:
                for j in range(wide):
                    columns = pl.ds(pl.multiple_of(panel * size + j * TW, TW), TW)
                    kept[rows, j * TW : (j + 1) * TW] = own_ref[:, columns] * flags[j].astype(kept.dtype)
                continue
            total = totals[offset]
            begins = {}
            for sign in (-1, 1):
                begins[sign] = sum(
                    (jnp.maximum(totals[sign * hop], 2 * SEND) for hop in range(1, abs(offset))), jnp.int32(0)
                )
            before = panel * firsts[offset]
            for j, flag in enumerate(flags):
                at = (begins[-1] + before, begins[1] + total - 1 - before)
                columns = slice(j * TW, (j + 1) * TW)
                if offset == far:
                    on_right = at[0] < cap
                    for side, take in ((0, on_right), (1, jnp.logical_not(on_right))):
                        index = jnp.clip(at[side] - begin, 0, stores[side].shape[0] - 1)

                        @pl.when(take)
                        def _():
                            kept[rows, columns] = stores[side][index] * flag.astype(kept.dtype)
                else:
                    side = 0 if offset < 0 else 1
                    valid = flag
                    index = jnp.clip(at[side] - begin, 0, stores[side].shape[0] - 1)
                    if slot < low:
                        valid = jnp.where(at[side] >= carried, flag, 0)
                        waiting += valid
                        leftover.append((rows, columns, side, index, valid))
                    else:
                        if limit is not None:
                            valid = jnp.where(at[side] < limit, flag, 0)
                        kept[rows, columns] = stores[side][index] * valid.astype(kept.dtype)
                before += flag
        late[0] = waiting
        if carry:

            @pl.when(waiting != 0)
            def _():
                for rows, columns, side, index, valid in leftover:
                    kept[rows, columns] = stores[side][index] * valid.astype(kept.dtype)


    height = a_ref.shape[1]
    row_count = height // STEPS_OF[final]

    def total_of(from_slot):
        for r in range(0, row_count, PIECE[0]):
            inner = pl.ds(pl.multiple_of(step * row_count + r, PIECE[0]), PIECE[0])
            parts = [a_ref[slot, inner, :] for slot in range(from_slot, high)]
            parts = jnp.concatenate(parts, axis=1) if len(parts) > 1 else parts[0]
            for c in range(0, size, PIECE[1]):
                across = pl.ds(pl.multiple_of(panel * size + c, PIECE[1]), PIECE[1])
                product = jnp.dot(
                    parts, kept[(from_slot - start) * depth :, c : c + PIECE[1]], preferred_element_type=jnp.float32
                )
                base = base_ref[r : r + PIECE[0], c : c + PIECE[1]] if low == 0 else base_ref[inner, across]
                total = base.astype(jnp.float32) + product
                if final:
                    done[inner, across] = total.astype(done.dtype)
                else:
                    out_ref[inner, across] = total
            if final:
                across = pl.ds(pl.multiple_of(panel * size, size), size)
                pltpu.make_async_copy(done.at[inner, across], out_ref.at[inner, across], written).start()

    if carry:

        @pl.when(late[0] != 0)
        def _():
            total_of(start)

        @pl.when(late[0] == 0)
        def _():
            total_of(low)

    else:
        total_of(low)

    if final:

        @pl.when((panel == pl.num_programs(0) - 1) & (step == pl.num_programs(1) - 1))
        def _():
            pltpu.make_async_copy(done, out_ref, written).wait()


def gather_multiply(
    place, b_mask, a_kept, own, sends, base, *, low, high, carry, carried, limit, offsets, sends_of, cap, width
):
    height, depth = a_kept.shape[1:]
    final = high == len(offsets)
    size = width // 2
    steps = STEPS_OF[final]
    rows = height // steps
    whole = pl.BlockSpec(memory_space=pltpu.VMEM)
    block = pl.BlockSpec((rows, size), lambda p, i, *_: (i, p))
    operands = [place, b_mask, a_kept]
    in_specs = [whole]
    if own is not None:
        operands.append(own)
        in_specs.append(whole)
    for side in range(2):
        arrays = [sends[index][side] for index in sends_of]
        operands += arrays
        in_specs += [whole] * len(arrays)
    store = pltpu.VMEM((max(1, sum(array.shape[0] for array in arrays)), depth, TW), jnp.bfloat16)
    operands.append(base)
    in_specs.append(whole if low else block)
    aliases = {}
    if final:
        out_shape = jax.ShapeDtypeStruct((height, width), jnp.bfloat16)
    else:
        out_shape = pltpu.VMEM((height, width), jnp.float32)
        if low:
            aliases = {len(operands) - 1: 0}
    return pl.pallas_call(
        functools.partial(
            gather_multiply_body, low=low, high=high, carry=carry, carried=carried, limit=limit, offsets=offsets,
            sends_of=sends_of, tiles=width // TW, cap=cap, own=own is not None, final=final,
        ),
        grid_spec=pltpu.PrefetchScalarGridSpec(
            num_scalar_prefetch=2,
            grid=(2, steps),
            in_specs=in_specs,
            out_specs=pl.BlockSpec(memory_space=pl.ANY) if final else whole,
            scratch_shapes=[
                pltpu.VMEM(((high - low + carry) * depth, size), jnp.bfloat16), store, store, pltpu.SMEM((1,), jnp.int32)
            ]
            + ([pltpu.VMEM((height, width), jnp.bfloat16), pltpu.SemaphoreType.DMA] if final else []),
        ),
        out_shape=out_shape,
        input_output_aliases=aliases,
        cost_estimate=pl.CostEstimate(flops=height * size * depth // 16, bytes_accessed=height * size // 16, transcendentals=0),
        compiler_params=pltpu.CompilerParams(vmem_limit_bytes=GATHER_VMEM),
    )(*operands)


def sparse(n, cap, a_tiles, b_tiles, a_mask, b_mask, c_given, plan, *heads):
    ring = ring_of(n)
    right = [(ring[i], ring[(i + 1) % n]) for i in range(n)]
    left = [(t, s) for s, t in right]
    height, width = c_given.shape
    far = n // 2
    panel = width // 2
    tiles = width // TW
    offsets, place = places(n, lax.axis_index("row"), lax.axis_index("col"), height)

    sizes = [SEND] * (cap // SEND) + ([cap % SEND] if cap % SEND else [])
    last = len(sizes)

    def sent_by(count):
        return min(-(-count // SEND), last)

    cut = 1 + 2 * ((far - 1) // 2)
    near, edge = 2 * far - 3, 2 * far - 1
    middle = (sent_by(tiles * (far - 2)) - 1) * SEND
    limit = (cap - 2) // SEND * SEND
    phases = [
        dict(low=0, high=1, carry=0, carried=0, limit=None, sends_of=()),
        dict(low=1, high=cut, carry=0, carried=0, limit=None, sends_of=(0, sent_by(tiles * (cut // 2)))),
        dict(low=cut, high=near, carry=0, carried=0, limit=middle, sends_of=(2 * (cut // 2), middle // SEND)),
        dict(
            low=near, high=edge, carry=near - cut, carried=middle, limit=limit,
            sends_of=(min(2 * (far - 2), middle // SEND), limit // SEND),
        ),
        dict(
            low=edge, high=n, carry=edge - near, carried=limit, limit=None,
            sends_of=(min(2 * (far - 1), limit // SEND), last),
        ),
    ]
    work = collections.defaultdict(list)
    for phase in phases:
        begin, end = phase["sends_of"] or (0, 2)
        phase["sends_of"] = tuple(range(begin, end)) if phase["low"] else ()
        work[min(end + 1, last)].append(phase)

    sends = []
    tied = []
    other = a_kept = total = None
    for index in range(last + 1):
        if index < last:
            if index == 0:
                sources = heads
            elif index == 1:
                packed = pack(b_mask, b_tiles, n, False)
                sources = packed[::2]
            else:
                arrays = []
                for side in range(2):
                    arrays += [packed[2 * side + 1] if index == 2 else sends[index - 3][side], sends[index - 2][side]]
                if tied:
                    *arrays, _ = lax.optimization_barrier((*arrays, tied))
                    tied = []
                sources = choose(plan, arrays, sizes[index])
            sends.append([lax.ppermute(source, "row", pairs) for source, pairs in zip(sources, (right, left))])
        if index == 0:
            other = lax.ppermute(a_tiles, "col", [(0, 1), (1, 0)])
        if index == 1:
            source = pltpu.with_memory_space_constraint(a_tiles, pltpu.HBM)
            a_kept = prepare(place, a_mask, source, other, n)
            tied.append(a_kept)
        for phase in work[index]:
            first = phase["low"] == 0
            total = gather_multiply(
                place, b_mask, a_kept, b_tiles if first else None, sends,
                pltpu.with_memory_space_constraint(c_given, pltpu.HBM) if first else total,
                offsets=tuple(offsets), cap=cap, width=width, **phase,
            )
            tied.append(total)
    return total


def on_device(n, *args):
    b_tiles, b_mask = args[1], args[3]
    *heads, plan = pack(b_mask, b_tiles, n, True)
    tiles = b_tiles.shape[1] // TW
    most = tiles * (n // 2 - 1) + tiles // 2
    caps = [most - most * saved // 28 for saved in (4, 3)]
    branches = [functools.partial(sparse, n, cap) for cap in caps]
    branches.append(lambda *operands: dense(n, *operands[:5]))
    which = sum((plan[0] > cap).astype(jnp.int32) for cap in caps)
    return lax.switch(which, branches, *args, plan, *heads)


def solution(mesh):
    return jax.shard_map(
        functools.partial(on_device, mesh.shape["row"]),
        mesh=mesh,
        in_specs=(
            P(("grp", "row"), "col"),
            P(("grp", "row"), "col"),
            P("grp", None),
            P("grp", None),
            P(("grp", "row"), "col"),
        ),
        out_specs=P(("grp", "row"), "col"),
        check_vma=False,
    )
```

```python
import collections
import functools

import jax
import jax.numpy as jnp
from jax import lax
from jax.experimental import pallas as pl
from jax.experimental.pallas import tpu as pltpu
from jax.sharding import PartitionSpec as P

TW = 256
ROWS = 512
LAST_ROWS = 1024
MIB = 1024 * 1024
VMEM = 20 * MIB
SEND = 3
GATHER_VMEM = 16 * MIB
STEPS_OF = {False: 2, True: 2}
PIECE = (256, 512)


def ring_of(n):
    if n == 8:
        return [0, 2, 4, 6, 7, 5, 3, 1]
    return list(range(n))


def prepare_body(place, a_mask, own_ref, other_ref, out_ref, *, depth, n):
    per_half = n // 2
    tiles = own_ref.shape[0] // TW
    for tile in range(tiles):
        rows = slice(tile * TW, (tile + 1) * TW)
        tile_row = place[0] + pl.program_id(0) * tiles + tile
        for away, ref in enumerate((own_ref, other_ref)):
            first = lax.rem(place[1] + away, 2) * per_half
            for index in range(per_half):
                owner = first + index
                flag = a_mask[tile_row, owner * depth // TW].astype(out_ref.dtype)
                out_ref[place[2 + n + owner], rows, :] = ref[rows, index * depth : (index + 1) * depth] * flag


def prepare(place, a_mask, own, other, n):
    height, half = own.shape
    depth = 2 * half // n
    return pl.pallas_call(
        functools.partial(prepare_body, depth=depth, n=n),
        grid_spec=pltpu.PrefetchScalarGridSpec(
            num_scalar_prefetch=2,
            grid=(height // ROWS,),
            in_specs=[pl.BlockSpec((ROWS, half), lambda i, *_: (i, 0))] * 2,
            out_specs=pl.BlockSpec((n, ROWS, depth), lambda i, *_: (0, i, 0)),
        ),
        out_shape=pltpu.VMEM((n, height, depth), jnp.bfloat16),
        cost_estimate=pl.CostEstimate(flops=0, bytes_accessed=height * half // 16, transcendentals=0),
        compiler_params=pltpu.CompilerParams(vmem_limit_bytes=VMEM),
    )(place, a_mask, own, other)


def multiply_body(place, b_mask, *refs, layout, low, high, first, chained):
    left, refs = refs[: high - low], refs[high - low :]
    blocks = refs[: len(layout)]
    base_ref = refs[len(layout)]
    out_ref, kept = refs[len(layout) + 1 + chained :]
    depth = blocks[0].shape[0]

    @pl.when(pl.program_id(0) == 0)
    def _():
        for ref, (slot, shift) in zip(blocks, layout):
            tile_k = place[2 + slot] * depth // TW
            for j in range(ref.shape[1] // TW):
                at = shift + j * TW
                flag = b_mask[tile_k, place[1] * 8 + (first + at) // TW].astype(kept.dtype)
                block = ref[:, j * TW : (j + 1) * TW]
                kept[(slot - low) * depth : (slot - low + 1) * depth, at : at + TW] = block * flag

    left = [ref[0] for ref in left]
    left = jnp.concatenate(left, axis=1) if len(left) > 1 else left[0]
    product = jnp.dot(left, kept[...], preferred_element_type=jnp.float32)
    out_ref[...] = (base_ref[...].astype(jnp.float32) + product).astype(out_ref.dtype)


def multiply(place, b_mask, a_kept, arrived, base, base_column, out, *, low, high, first, size, wide, width):
    height = a_kept.shape[1]
    depth = arrived[0][2].shape[0]
    rows = LAST_ROWS if high - low == 1 else ROWS
    operands = [place, b_mask] + [a_kept] * (high - low)
    whole = pl.BlockSpec(memory_space=pltpu.VMEM)
    in_specs = [
        pl.BlockSpec((1, rows, depth), functools.partial(lambda slot, i, *_: (slot, i, 0), slot)) for slot in range(low, high)
    ]
    for _, _, array in arrived:
        operands.append(array)
        if array.shape[1] == width:
            in_specs.append(pl.BlockSpec((depth, size), lambda i, *_: (0, first // size)))
        else:
            in_specs.append(whole)
    operands.append(base)
    in_specs.append(pl.BlockSpec((rows, size), lambda i, *_: (i, base_column // size)))
    if wide:
        out_shape = pltpu.VMEM((height, size), jnp.float32)
        out_spec = pl.BlockSpec((rows, size), lambda i, *_: (i, 0))
    else:
        out_shape = jax.ShapeDtypeStruct((height, width), jnp.bfloat16)
        out_spec = pl.BlockSpec((rows, size), lambda i, *_: (i, first // size))
    aliases = {}
    if out is not None:
        aliases = {len(operands): 0}
        operands.append(pltpu.with_memory_space_constraint(out, pltpu.HBM))
        in_specs.append(pl.BlockSpec(memory_space=pl.ANY))
    extent = (high - low) * depth
    return pl.pallas_call(
        functools.partial(
            multiply_body,
            layout=tuple((slot, shift) for slot, shift, _ in arrived),
            low=low,
            high=high,
            first=first,
            chained=out is not None,
        ),
        grid_spec=pltpu.PrefetchScalarGridSpec(
            num_scalar_prefetch=2,
            grid=(height // rows,),
            in_specs=in_specs,
            out_specs=out_spec,
            scratch_shapes=[pltpu.VMEM((extent, size), jnp.bfloat16)],
        ),
        out_shape=out_shape,
        input_output_aliases=aliases,
        cost_estimate=pl.CostEstimate(
            flops=height * size * extent // 16, bytes_accessed=height * size // 16, transcendentals=0
        ),
        compiler_params=pltpu.CompilerParams(vmem_limit_bytes=VMEM),
    )(*operands)


def places(n, row, col, height):
    ring = ring_of(n)
    far = n // 2
    offsets = [0] + [sign * hop for hop in range(1, far) for sign in (-1, 1)] + [far]
    table = []
    for r in range(n):
        owners = [ring[(ring.index(r) + o) % n] for o in offsets]
        table.append(owners + [owners.index(owner) for owner in range(n)])
    table = lax.dynamic_index_in_dim(jnp.array(table, jnp.int32), row, 0, keepdims=False)
    return offsets, jnp.concatenate([jnp.stack([row * (height // TW), col]).astype(jnp.int32), table])


def dense(n, a_tiles, b_tiles, a_mask, b_mask, c_given):
    ring = ring_of(n)
    right = [(ring[i], ring[(i + 1) % n]) for i in range(n)]
    left = [(t, s) for s, t in right]
    row = lax.axis_index("row")
    col = lax.axis_index("col")
    height, width = c_given.shape
    far = n // 2
    panel = width // 2

    offsets, place = places(n, row, col, height)

    rounds = [(p, hop, 0, panel) for hop in range(1, far) for p in range(2)]
    rounds += [(0, far, 0, panel), (1, far, 0, panel)]
    work = collections.defaultdict(list)
    last = len(rounds)
    work[last - 4] = [(0, 0, n - 3, 0, panel)]
    work[last - 3] = [(1, 0, n - 3, 0, panel)]
    work[last - 2] = [(0, n - 3, n - 1, 0, panel)]
    work[last] = [(1, n - 3, n - 1, 0, panel), (0, n - 1, n, 0, panel), (1, n - 1, n, 0, panel)]

    blocks = [{0: b_tiles} for _ in range(2)]
    other = a_kept = out = None
    wide = {}
    tied = []
    for index in range(last + 1):
        if index < last:
            p, hop, start, stop = rounds[index]
            sources = []
            for sign in (-1, 1):
                if hop == 1:
                    source = b_tiles[:, p * panel : (p + 1) * panel]
                else:
                    source = blocks[p][sign * (hop - 1)]
                if hop == far:
                    middle = (start + stop) // 2
                    source = source[:, start:middle] if sign < 0 else source[:, middle:stop]
                sources.append(source)
            if tied:
                *sources, _ = lax.optimization_barrier((*sources, tied))
            tied = []
            for sign, pairs, source in zip((-1, 1), (right, left), sources):
                key = (sign * hop, start) if hop == far else sign * hop
                blocks[p][key] = lax.ppermute(source, "row", pairs)
        if index == 0:
            other = lax.ppermute(a_tiles, "col", [(0, 1), (1, 0)])
        if index == 1:
            source = pltpu.with_memory_space_constraint(a_tiles, pltpu.HBM)
            a_kept = prepare(place, a_mask, source, other, n)
            tied.append(a_kept)
        for p, low, high, start, stop in work[index]:
            arrived = []
            for slot in range(low, high):
                if offsets[slot] == far:
                    arrived.append((slot, 0, blocks[p][-far, start]))
                    arrived.append((slot, (stop - start) // 2, blocks[p][far, start]))
                else:
                    arrived.append((slot, 0, blocks[p][offsets[slot]]))
            done = high == n
            if low:
                base, base_column = wide[p], start
            else:
                base, base_column = pltpu.with_memory_space_constraint(c_given, pltpu.HBM), p * panel + start
            result = multiply(
                place, b_mask, a_kept, arrived, base, base_column, out if done else None,
                low=low, high=high, first=p * panel + start, size=stop - start, wide=not done, width=width,
            )
            tied.append(result)
            if done:
                out = result
            else:
                wide[p] = result
    return out


def pack_body(mask_ref, b_ref, *refs, n, tiles, head):
    depth = b_ref.shape[0]
    arrived = refs[-1]
    if head:
        b_mask, block, read = refs[3:6]
        reads = [pltpu.make_async_copy(mask_ref, b_mask, read), pltpu.make_async_copy(b_ref, block, arrived)]
        for copy in reads:
            copy.start()
        reads[0].wait()
    else:
        b_mask = mask_ref
    mine = lax.axis_index("row") * depth // TW
    half = lax.axis_index("col") * tiles
    flags = [b_mask[mine, half + j] for j in range(tiles)]
    total = sum(flags)
    end = jnp.maximum(total, 2 * SEND)

    def put(ref, low, j, at):
        @pl.when((at >= low) & (at < low + SEND))
        def _():
            pltpu.make_async_copy(b_ref.at[:, j * TW : (j + 1) * TW], ref.at[at - low], arrived).start()

    firsts = []
    before = jnp.int32(0)
    for j in range(tiles):
        dropped = total + j - before
        places = (jnp.where(flags[j] != 0, before, dropped), jnp.where(flags[j] != 0, total - 1 - before, dropped))
        for side, at in enumerate(places):
            if head:
                firsts.append((refs[side], j, at))
            else:
                put(refs[2 * side], SEND, j, at)
                put(refs[2 * side + 1], end - SEND, j, at)
        before += flags[j]

    if head:
        plan = refs[2]
        ring = ring_of(n)
        far = n // 2
        need = jnp.int32(0)
        for c in range(2):
            kept = []
            for owner in ring:
                count = jnp.int32(0)
                for j in range(tiles):
                    count += b_mask[owner * depth // TW, c * tiles + j]
                kept.append(count)
            span = [jnp.maximum(count, 2 * SEND) for count in kept]
            for q in range(n):
                right = sum(span[(q - hop) % n] for hop in range(1, far))
                left = sum(span[(q + hop) % n] for hop in range(1, far))
                both = lax.shift_right_logical(right + left + kept[(q + far) % n] + 1, 1)
                need = jnp.maximum(need, jnp.maximum(jnp.maximum(right, left), both))
        plan[0] = need
        plan[1] = 3 * SEND - end
        reads[1].wait()
        for ref, j, at in firsts:

            @pl.when(at < SEND)
            def _():
                ref[at] = block[:, j * TW : (j + 1) * TW]

    else:
        for ref in refs[:4]:
            pltpu.make_async_copy(ref, ref, arrived).wait()


def pack(b_mask, b_tiles, n, head):
    depth, width = b_tiles.shape
    whole = pl.BlockSpec(memory_space=pltpu.VMEM)
    count = 2 if head else 4
    out_shape = [pltpu.VMEM((SEND, depth, TW), jnp.bfloat16)] * count
    out_specs = [whole] * count
    scratch = []
    if head:
        scratch = [pltpu.SMEM(b_mask.shape, jnp.int32), pltpu.VMEM((depth, width), jnp.bfloat16), pltpu.SemaphoreType.DMA]
        out_shape.append(jax.ShapeDtypeStruct((2,), jnp.int32))
        out_specs.append(pl.BlockSpec(memory_space=pltpu.SMEM))
    return pl.pallas_call(
        functools.partial(pack_body, n=n, tiles=width // TW, head=head),
        grid_spec=pltpu.PrefetchScalarGridSpec(
            num_scalar_prefetch=0 if head else 1,
            grid=(1,),
            in_specs=[pl.BlockSpec(memory_space=pl.ANY)] * (2 if head else 1),
            out_specs=out_specs,
            scratch_shapes=scratch + [pltpu.SemaphoreType.DMA],
        ),
        out_shape=out_shape,
        cost_estimate=pl.CostEstimate(flops=0, bytes_accessed=1024, transcendentals=0),
        compiler_params=pltpu.CompilerParams(vmem_limit_bytes=VMEM),
    )(b_mask, pltpu.with_memory_space_constraint(b_tiles, pltpu.HBM))


def choose_body(plan, *refs, count):
    for before, last, out in (refs[0:2] + refs[4:5], refs[2:4] + refs[5:6]):
        for start in range(1, SEND + 1):

            @pl.when(plan[1] == start)
            def _():
                for i in range(count):
                    at = start + i
                    out[i] = before[at] if at < SEND else last[at - SEND]


def choose(plan, arrays, count):
    shape = (count,) + arrays[0].shape[1:]
    whole = pl.BlockSpec(memory_space=pltpu.VMEM)
    return pl.pallas_call(
        functools.partial(choose_body, count=count),
        grid_spec=pltpu.PrefetchScalarGridSpec(
            num_scalar_prefetch=1, grid=(1,), in_specs=[whole] * 4, out_specs=[whole] * 2
        ),
        out_shape=[pltpu.VMEM(shape, jnp.bfloat16)] * 2,
        cost_estimate=pl.CostEstimate(flops=0, bytes_accessed=1024, transcendentals=0),
        compiler_params=pltpu.CompilerParams(vmem_limit_bytes=VMEM),
    )(plan, *arrays)


def gather_multiply_body(
    place, b_mask, *refs, low, high, carry, carried, limit, offsets, sends_of, tiles, cap, own, final
):
    a_ref, refs = refs[0], refs[1:]
    own_ref, refs = (refs[0], refs[1:]) if own else (None, refs)
    count = len(sends_of)
    sends = (refs[:count], refs[count : 2 * count])
    base_ref, out_ref, kept, store_right, store_left, late, *rest = refs[2 * count :]
    done, written = rest if final else (None, None)
    stores = (store_right, store_left)
    depth = a_ref.shape[2]
    size = kept.shape[1]
    far = max(offsets)
    panel, step = pl.program_id(0), pl.program_id(1)
    begin = sends_of[0] * SEND if sends_of else 0
    start = low - carry
    wide = size // TW

    @pl.when((panel == 0) & (step == 0))
    def _():
        for side in range(2):
            at = 0
            for ref in sends[side]:
                stores[side][at : at + ref.shape[0]] = ref[...]
                at += ref.shape[0]

    @pl.when(step == 0)
    def _():
        def row_of(slot):
            return place[2 + slot] * depth // TW

        totals = {}
        firsts = {}
        for slot, offset in enumerate(offsets[:high]):
            flags = [b_mask[row_of(slot), place[1] * tiles + j] for j in range(tiles)]
            firsts[offset] = sum(flags[:wide])
            totals[offset] = firsts[offset] + sum(flags[wide:])
        waiting = jnp.int32(0)
        leftover = []
        for slot in range(start, high):
            rows = slice((slot - start) * depth, (slot - start + 1) * depth)
            offset = offsets[slot]
            flags = [b_mask[row_of(slot), place[1] * tiles + panel * wide + j] for j in range(wide)]
            if offset == 0:
                for j in range(wide):
                    columns = pl.ds(pl.multiple_of(panel * size + j * TW, TW), TW)
                    kept[rows, j * TW : (j + 1) * TW] = own_ref[:, columns] * flags[j].astype(kept.dtype)
                continue
            total = totals[offset]
            begins = {}
            for sign in (-1, 1):
                begins[sign] = sum(
                    (jnp.maximum(totals[sign * hop], 2 * SEND) for hop in range(1, abs(offset))), jnp.int32(0)
                )
            before = panel * firsts[offset]
            for j, flag in enumerate(flags):
                at = (begins[-1] + before, begins[1] + total - 1 - before)
                columns = slice(j * TW, (j + 1) * TW)
                if offset == far:
                    on_right = at[0] < cap
                    for side, take in ((0, on_right), (1, jnp.logical_not(on_right))):
                        index = jnp.clip(at[side] - begin, 0, stores[side].shape[0] - 1)

                        @pl.when(take)
                        def _():
                            kept[rows, columns] = stores[side][index] * flag.astype(kept.dtype)
                else:
                    side = 0 if offset < 0 else 1
                    valid = flag
                    index = jnp.clip(at[side] - begin, 0, stores[side].shape[0] - 1)
                    if slot < low:
                        valid = jnp.where(at[side] >= carried, flag, 0)
                        waiting += valid
                        leftover.append((rows, columns, side, index, valid))
                    else:
                        if limit is not None:
                            valid = jnp.where(at[side] < limit, flag, 0)
                        kept[rows, columns] = stores[side][index] * valid.astype(kept.dtype)
                before += flag
        late[0] = waiting
        if carry:

            @pl.when(waiting != 0)
            def _():
                for rows, columns, side, index, valid in leftover:
                    kept[rows, columns] = stores[side][index] * valid.astype(kept.dtype)


    height = a_ref.shape[1]
    row_count = height // STEPS_OF[final]

    def total_of(from_slot):
        for r in range(0, row_count, PIECE[0]):
            inner = pl.ds(pl.multiple_of(step * row_count + r, PIECE[0]), PIECE[0])
            parts = [a_ref[slot, inner, :] for slot in range(from_slot, high)]
            parts = jnp.concatenate(parts, axis=1) if len(parts) > 1 else parts[0]
            for c in range(0, size, PIECE[1]):
                across = pl.ds(pl.multiple_of(panel * size + c, PIECE[1]), PIECE[1])
                product = jnp.dot(
                    parts, kept[(from_slot - start) * depth :, c : c + PIECE[1]], preferred_element_type=jnp.float32
                )
                base = base_ref[r : r + PIECE[0], c : c + PIECE[1]] if low == 0 else base_ref[inner, across]
                total = base.astype(jnp.float32) + product
                if final:
                    done[inner, across] = total.astype(done.dtype)
                else:
                    out_ref[inner, across] = total
            if final:
                across = pl.ds(pl.multiple_of(panel * size, size), size)
                pltpu.make_async_copy(done.at[inner, across], out_ref.at[inner, across], written).start()

    if carry:

        @pl.when(late[0] != 0)
        def _():
            total_of(start)

        @pl.when(late[0] == 0)
        def _():
            total_of(low)

    else:
        total_of(low)

    if final:

        @pl.when((panel == pl.num_programs(0) - 1) & (step == pl.num_programs(1) - 1))
        def _():
            pltpu.make_async_copy(done, out_ref, written).wait()


def gather_multiply(
    place, b_mask, a_kept, own, sends, base, *, low, high, carry, carried, limit, offsets, sends_of, cap, width
):
    height, depth = a_kept.shape[1:]
    final = high == len(offsets)
    size = width // 2
    steps = STEPS_OF[final]
    rows = height // steps
    whole = pl.BlockSpec(memory_space=pltpu.VMEM)
    block = pl.BlockSpec((rows, size), lambda p, i, *_: (i, p))
    operands = [place, b_mask, a_kept]
    in_specs = [whole]
    if own is not None:
        operands.append(own)
        in_specs.append(whole)
    for side in range(2):
        arrays = [sends[index][side] for index in sends_of]
        operands += arrays
        in_specs += [whole] * len(arrays)
    store = pltpu.VMEM((max(1, sum(array.shape[0] for array in arrays)), depth, TW), jnp.bfloat16)
    operands.append(base)
    in_specs.append(whole if low else block)
    aliases = {}
    if final:
        out_shape = jax.ShapeDtypeStruct((height, width), jnp.bfloat16)
    else:
        out_shape = pltpu.VMEM((height, width), jnp.float32)
        if low:
            aliases = {len(operands) - 1: 0}
    return pl.pallas_call(
        functools.partial(
            gather_multiply_body, low=low, high=high, carry=carry, carried=carried, limit=limit, offsets=offsets,
            sends_of=sends_of, tiles=width // TW, cap=cap, own=own is not None, final=final,
        ),
        grid_spec=pltpu.PrefetchScalarGridSpec(
            num_scalar_prefetch=2,
            grid=(2, steps),
            in_specs=in_specs,
            out_specs=pl.BlockSpec(memory_space=pl.ANY) if final else whole,
            scratch_shapes=[
                pltpu.VMEM(((high - low + carry) * depth, size), jnp.bfloat16), store, store, pltpu.SMEM((1,), jnp.int32)
            ]
            + ([pltpu.VMEM((height, width), jnp.bfloat16), pltpu.SemaphoreType.DMA] if final else []),
        ),
        out_shape=out_shape,
        input_output_aliases=aliases,
        cost_estimate=pl.CostEstimate(flops=height * size * depth // 16, bytes_accessed=height * size // 16, transcendentals=0),
        compiler_params=pltpu.CompilerParams(vmem_limit_bytes=GATHER_VMEM),
    )(*operands)


def sparse(n, cap, a_tiles, b_tiles, a_mask, b_mask, c_given, plan, *heads):
    ring = ring_of(n)
    right = [(ring[i], ring[(i + 1) % n]) for i in range(n)]
    left = [(t, s) for s, t in right]
    height, width = c_given.shape
    far = n // 2
    panel = width // 2
    tiles = width // TW
    offsets, place = places(n, lax.axis_index("row"), lax.axis_index("col"), height)

    sizes = [SEND] * (cap // SEND) + ([cap % SEND] if cap % SEND else [])
    last = len(sizes)

    def sent_by(count):
        return min(-(-count // SEND), last)

    cut = 1 + 2 * ((far - 1) // 2)
    near, edge = 2 * far - 3, 2 * far - 1
    middle = (sent_by(tiles * (far - 2)) - 1) * SEND
    limit = (cap - 2) // SEND * SEND
    phases = [
        dict(low=0, high=1, carry=0, carried=0, limit=None, sends_of=()),
        dict(low=1, high=cut, carry=0, carried=0, limit=None, sends_of=(0, sent_by(tiles * (cut // 2)))),
        dict(low=cut, high=near, carry=0, carried=0, limit=middle, sends_of=(2 * (cut // 2), middle // SEND)),
        dict(
            low=near, high=edge, carry=near - cut, carried=middle, limit=limit,
            sends_of=(min(2 * (far - 2), middle // SEND), limit // SEND),
        ),
        dict(
            low=edge, high=n, carry=edge - near, carried=limit, limit=None,
            sends_of=(min(2 * (far - 1), limit // SEND), last),
        ),
    ]
    work = collections.defaultdict(list)
    for phase in phases:
        begin, end = phase["sends_of"] or (0, 2)
        phase["sends_of"] = tuple(range(begin, end)) if phase["low"] else ()
        work[min(end + 1, last)].append(phase)

    sends = []
    tied = []
    other = a_kept = total = None
    for index in range(last + 1):
        if index < last:
            if index == 0:
                sources = heads
            elif index == 1:
                packed = pack(b_mask, b_tiles, n, False)
                sources = packed[::2]
            else:
                arrays = []
                for side in range(2):
                    arrays += [packed[2 * side + 1] if index == 2 else sends[index - 3][side], sends[index - 2][side]]
                if tied:
                    *arrays, _ = lax.optimization_barrier((*arrays, tied))
                    tied = []
                sources = choose(plan, arrays, sizes[index])
            sends.append([lax.ppermute(source, "row", pairs) for source, pairs in zip(sources, (right, left))])
        if index == 0:
            other = lax.ppermute(a_tiles, "col", [(0, 1), (1, 0)])
        if index == 1:
            source = pltpu.with_memory_space_constraint(a_tiles, pltpu.HBM)
            a_kept = prepare(place, a_mask, source, other, n)
            tied.append(a_kept)
        for phase in work[index]:
            first = phase["low"] == 0
            total = gather_multiply(
                place, b_mask, a_kept, b_tiles if first else None, sends,
                pltpu.with_memory_space_constraint(c_given, pltpu.HBM) if first else total,
                offsets=tuple(offsets), cap=cap, width=width, **phase,
            )
            tied.append(total)
    return total


def on_device(n, *args):
    b_tiles, b_mask = args[1], args[3]
    *heads, plan = pack(b_mask, b_tiles, n, True)
    tiles = b_tiles.shape[1] // TW
    most = tiles * (n // 2 - 1) + tiles // 2
    caps = [most - most * saved // 28 for saved in (4, 3)]
    branches = [functools.partial(sparse, n, cap) for cap in caps]
    branches.append(lambda *operands: dense(n, *operands[:5]))
    which = sum((plan[0] > cap).astype(jnp.int32) for cap in caps)
    return lax.switch(which, branches, *args, plan, *heads)


def solution(mesh):
    return jax.shard_map(
        functools.partial(on_device, mesh.shape["row"]),
        mesh=mesh,
        in_specs=(
            P(("grp", "row"), "col"),
            P(("grp", "row"), "col"),
            P("grp", None),
            P("grp", None),
            P(("grp", "row"), "col"),
        ),
        out_specs=P(("grp", "row"), "col"),
        check_vma=False,
    )
```

```python
import collections
import functools

import jax
import jax.numpy as jnp
from jax import lax
from jax.experimental import pallas as pl
from jax.experimental.pallas import tpu as pltpu
from jax.sharding import PartitionSpec as P

TW = 256
ROWS = 512
LAST_ROWS = 1024
MIB = 1024 * 1024
VMEM = 20 * MIB
SEND = 3
GATHER_VMEM = 16 * MIB
STEPS_OF = {False: 2, True: 2}
PIECE = (256, 512)


def ring_of(n):
    if n == 8:
        return [0, 2, 4, 6, 7, 5, 3, 1]
    return list(range(n))


def prepare_body(place, a_mask, own_ref, other_ref, out_ref, *, depth, n):
    per_half = n // 2
    tiles = own_ref.shape[0] // TW
    for tile in range(tiles):
        rows = slice(tile * TW, (tile + 1) * TW)
        tile_row = place[0] + pl.program_id(0) * tiles + tile
        for away, ref in enumerate((own_ref, other_ref)):
            first = lax.rem(place[1] + away, 2) * per_half
            for index in range(per_half):
                owner = first + index
                flag = a_mask[tile_row, owner * depth // TW].astype(out_ref.dtype)
                out_ref[place[2 + n + owner], rows, :] = ref[rows, index * depth : (index + 1) * depth] * flag


def prepare(place, a_mask, own, other, n):
    height, half = own.shape
    depth = 2 * half // n
    return pl.pallas_call(
        functools.partial(prepare_body, depth=depth, n=n),
        grid_spec=pltpu.PrefetchScalarGridSpec(
            num_scalar_prefetch=2,
            grid=(height // ROWS,),
            in_specs=[pl.BlockSpec((ROWS, half), lambda i, *_: (i, 0))] * 2,
            out_specs=pl.BlockSpec((n, ROWS, depth), lambda i, *_: (0, i, 0)),
        ),
        out_shape=pltpu.VMEM((n, height, depth), jnp.bfloat16),
        cost_estimate=pl.CostEstimate(flops=0, bytes_accessed=height * half // 16, transcendentals=0),
        compiler_params=pltpu.CompilerParams(vmem_limit_bytes=VMEM),
    )(place, a_mask, own, other)


def multiply_body(place, b_mask, *refs, layout, low, high, first, chained):
    left, refs = refs[: high - low], refs[high - low :]
    blocks = refs[: len(layout)]
    base_ref = refs[len(layout)]
    out_ref, kept = refs[len(layout) + 1 + chained :]
    depth = blocks[0].shape[0]

    @pl.when(pl.program_id(0) == 0)
    def _():
        for ref, (slot, shift) in zip(blocks, layout):
            tile_k = place[2 + slot] * depth // TW
            for j in range(ref.shape[1] // TW):
                at = shift + j * TW
                flag = b_mask[tile_k, place[1] * 8 + (first + at) // TW].astype(kept.dtype)
                block = ref[:, j * TW : (j + 1) * TW]
                kept[(slot - low) * depth : (slot - low + 1) * depth, at : at + TW] = block * flag

    left = [ref[0] for ref in left]
    left = jnp.concatenate(left, axis=1) if len(left) > 1 else left[0]
    product = jnp.dot(left, kept[...], preferred_element_type=jnp.float32)
    out_ref[...] = (base_ref[...].astype(jnp.float32) + product).astype(out_ref.dtype)


def multiply(place, b_mask, a_kept, arrived, base, base_column, out, *, low, high, first, size, wide, width):
    height = a_kept.shape[1]
    depth = arrived[0][2].shape[0]
    rows = LAST_ROWS if high - low == 1 else ROWS
    operands = [place, b_mask] + [a_kept] * (high - low)
    whole = pl.BlockSpec(memory_space=pltpu.VMEM)
    in_specs = [
        pl.BlockSpec((1, rows, depth), functools.partial(lambda slot, i, *_: (slot, i, 0), slot)) for slot in range(low, high)
    ]
    for _, _, array in arrived:
        operands.append(array)
        if array.shape[1] == width:
            in_specs.append(pl.BlockSpec((depth, size), lambda i, *_: (0, first // size)))
        else:
            in_specs.append(whole)
    operands.append(base)
    in_specs.append(pl.BlockSpec((rows, size), lambda i, *_: (i, base_column // size)))
    if wide:
        out_shape = pltpu.VMEM((height, size), jnp.float32)
        out_spec = pl.BlockSpec((rows, size), lambda i, *_: (i, 0))
    else:
        out_shape = jax.ShapeDtypeStruct((height, width), jnp.bfloat16)
        out_spec = pl.BlockSpec((rows, size), lambda i, *_: (i, first // size))
    aliases = {}
    if out is not None:
        aliases = {len(operands): 0}
        operands.append(pltpu.with_memory_space_constraint(out, pltpu.HBM))
        in_specs.append(pl.BlockSpec(memory_space=pl.ANY))
    extent = (high - low) * depth
    return pl.pallas_call(
        functools.partial(
            multiply_body,
            layout=tuple((slot, shift) for slot, shift, _ in arrived),
            low=low,
            high=high,
            first=first,
            chained=out is not None,
        ),
        grid_spec=pltpu.PrefetchScalarGridSpec(
            num_scalar_prefetch=2,
            grid=(height // rows,),
            in_specs=in_specs,
            out_specs=out_spec,
            scratch_shapes=[pltpu.VMEM((extent, size), jnp.bfloat16)],
        ),
        out_shape=out_shape,
        input_output_aliases=aliases,
        cost_estimate=pl.CostEstimate(
            flops=height * size * extent // 16, bytes_accessed=height * size // 16, transcendentals=0
        ),
        compiler_params=pltpu.CompilerParams(vmem_limit_bytes=VMEM),
    )(*operands)


def places(n, row, col, height):
    ring = ring_of(n)
    far = n // 2
    offsets = [0] + [sign * hop for hop in range(1, far) for sign in (-1, 1)] + [far]
    table = []
    for r in range(n):
        owners = [ring[(ring.index(r) + o) % n] for o in offsets]
        table.append(owners + [owners.index(owner) for owner in range(n)])
    table = lax.dynamic_index_in_dim(jnp.array(table, jnp.int32), row, 0, keepdims=False)
    return offsets, jnp.concatenate([jnp.stack([row * (height // TW), col]).astype(jnp.int32), table])


def dense(n, a_tiles, b_tiles, a_mask, b_mask, c_given):
    ring = ring_of(n)
    right = [(ring[i], ring[(i + 1) % n]) for i in range(n)]
    left = [(t, s) for s, t in right]
    row = lax.axis_index("row")
    col = lax.axis_index("col")
    height, width = c_given.shape
    far = n // 2
    panel = width // 2

    offsets, place = places(n, row, col, height)

    rounds = [(p, hop, 0, panel) for hop in range(1, far) for p in range(2)]
    rounds += [(0, far, 0, panel), (1, far, 0, panel)]
    work = collections.defaultdict(list)
    last = len(rounds)
    work[last - 4] = [(0, 0, n - 3, 0, panel)]
    work[last - 3] = [(1, 0, n - 3, 0, panel)]
    work[last - 2] = [(0, n - 3, n - 1, 0, panel)]
    work[last] = [(1, n - 3, n - 1, 0, panel), (0, n - 1, n, 0, panel), (1, n - 1, n, 0, panel)]

    blocks = [{0: b_tiles} for _ in range(2)]
    other = a_kept = out = None
    wide = {}
    tied = []
    for index in range(last + 1):
        if index < last:
            p, hop, start, stop = rounds[index]
            sources = []
            for sign in (-1, 1):
                if hop == 1:
                    source = b_tiles[:, p * panel : (p + 1) * panel]
                else:
                    source = blocks[p][sign * (hop - 1)]
                if hop == far:
                    middle = (start + stop) // 2
                    source = source[:, start:middle] if sign < 0 else source[:, middle:stop]
                sources.append(source)
            if tied:
                *sources, _ = lax.optimization_barrier((*sources, tied))
            tied = []
            for sign, pairs, source in zip((-1, 1), (right, left), sources):
                key = (sign * hop, start) if hop == far else sign * hop
                blocks[p][key] = lax.ppermute(source, "row", pairs)
        if index == 0:
            other = lax.ppermute(a_tiles, "col", [(0, 1), (1, 0)])
        if index == 1:
            source = pltpu.with_memory_space_constraint(a_tiles, pltpu.HBM)
            a_kept = prepare(place, a_mask, source, other, n)
            tied.append(a_kept)
        for p, low, high, start, stop in work[index]:
            arrived = []
            for slot in range(low, high):
                if offsets[slot] == far:
                    arrived.append((slot, 0, blocks[p][-far, start]))
                    arrived.append((slot, (stop - start) // 2, blocks[p][far, start]))
                else:
                    arrived.append((slot, 0, blocks[p][offsets[slot]]))
            done = high == n
            if low:
                base, base_column = wide[p], start
            else:
                base, base_column = pltpu.with_memory_space_constraint(c_given, pltpu.HBM), p * panel + start
            result = multiply(
                place, b_mask, a_kept, arrived, base, base_column, out if done else None,
                low=low, high=high, first=p * panel + start, size=stop - start, wide=not done, width=width,
            )
            tied.append(result)
            if done:
                out = result
            else:
                wide[p] = result
    return out


def pack_body(mask_ref, b_ref, *refs, n, tiles, head):
    depth = b_ref.shape[0]
    arrived = refs[-1]
    b_mask, block, read = refs[-4:-1]
    reads = [pltpu.make_async_copy(mask_ref, b_mask, read), pltpu.make_async_copy(b_ref, block, arrived)]
    for copy in reads:
        copy.start()
    reads[0].wait()
    mine = lax.axis_index("row") * depth // TW
    half = lax.axis_index("col") * tiles
    flags = [b_mask[mine, half + j] for j in range(tiles)]
    total = sum(flags)
    end = jnp.maximum(total, 2 * SEND)

    firsts = []
    before = jnp.int32(0)
    for j in range(tiles):
        dropped = total + j - before
        places = (jnp.where(flags[j] != 0, before, dropped), jnp.where(flags[j] != 0, total - 1 - before, dropped))
        for side, at in enumerate(places):
            if head:
                firsts.append((refs[side], 0, j, at))
            else:
                firsts.append((refs[2 * side], SEND, j, at))
                firsts.append((refs[2 * side + 1], end - SEND, j, at))
        before += flags[j]

    if head:
        plan = refs[2]
        ring = ring_of(n)
        far = n // 2
        need = jnp.int32(0)
        for c in range(2):
            kept = []
            for owner in ring:
                count = jnp.int32(0)
                for j in range(tiles):
                    count += b_mask[owner * depth // TW, c * tiles + j]
                kept.append(count)
            span = [jnp.maximum(count, 2 * SEND) for count in kept]
            for q in range(n):
                right = sum(span[(q - hop) % n] for hop in range(1, far))
                left = sum(span[(q + hop) % n] for hop in range(1, far))
                both = lax.shift_right_logical(right + left + kept[(q + far) % n] + 1, 1)
                need = jnp.maximum(need, jnp.maximum(jnp.maximum(right, left), both))
        plan[0] = need
        plan[1] = 3 * SEND - end
    reads[1].wait()
    for ref, low, j, at in firsts:

        @pl.when((at >= low) & (at < low + SEND))
        def _():
            ref[at - low] = block[:, j * TW : (j + 1) * TW]


def pack(b_mask, b_tiles, n, head):
    depth, width = b_tiles.shape
    whole = pl.BlockSpec(memory_space=pltpu.VMEM)
    count = 2 if head else 4
    out_shape = [pltpu.VMEM((SEND, depth, TW), jnp.bfloat16)] * count
    out_specs = [whole] * count
    scratch = [pltpu.SMEM(b_mask.shape, jnp.int32), pltpu.VMEM((depth, width), jnp.bfloat16), pltpu.SemaphoreType.DMA]
    if head:
        out_shape.append(jax.ShapeDtypeStruct((2,), jnp.int32))
        out_specs.append(pl.BlockSpec(memory_space=pltpu.SMEM))
    return pl.pallas_call(
        functools.partial(pack_body, n=n, tiles=width // TW, head=head),
        grid_spec=pltpu.PrefetchScalarGridSpec(
            num_scalar_prefetch=0,
            grid=(1,),
            in_specs=[pl.BlockSpec(memory_space=pl.ANY)] * 2,
            out_specs=out_specs,
            scratch_shapes=scratch + [pltpu.SemaphoreType.DMA],
        ),
        out_shape=out_shape,
        cost_estimate=pl.CostEstimate(flops=0, bytes_accessed=1024, transcendentals=0),
        compiler_params=pltpu.CompilerParams(vmem_limit_bytes=VMEM),
    )(b_mask, pltpu.with_memory_space_constraint(b_tiles, pltpu.HBM))


def choose_body(plan, *refs, count):
    for before, last, out in (refs[0:2] + refs[4:5], refs[2:4] + refs[5:6]):
        for start in range(1, SEND + 1):

            @pl.when(plan[1] == start)
            def _():
                for i in range(count):
                    at = start + i
                    out[i] = before[at] if at < SEND else last[at - SEND]


def choose(plan, arrays, count):
    shape = (count,) + arrays[0].shape[1:]
    whole = pl.BlockSpec(memory_space=pltpu.VMEM)
    return pl.pallas_call(
        functools.partial(choose_body, count=count),
        grid_spec=pltpu.PrefetchScalarGridSpec(
            num_scalar_prefetch=1, grid=(1,), in_specs=[whole] * 4, out_specs=[whole] * 2
        ),
        out_shape=[pltpu.VMEM(shape, jnp.bfloat16)] * 2,
        cost_estimate=pl.CostEstimate(flops=0, bytes_accessed=1024, transcendentals=0),
        compiler_params=pltpu.CompilerParams(vmem_limit_bytes=VMEM),
    )(plan, *arrays)


def gather_multiply_body(
    place, b_mask, *refs, low, high, carry, carried, limit, offsets, sends_of, tiles, cap, own, final
):
    a_ref, refs = refs[0], refs[1:]
    own_ref, refs = (refs[0], refs[1:]) if own else (None, refs)
    count = len(sends_of)
    sends = (refs[:count], refs[count : 2 * count])
    base_ref, out_ref, kept, store_right, store_left, late, *rest = refs[2 * count :]
    done, written = rest if final else (None, None)
    stores = (store_right, store_left)
    depth = a_ref.shape[2]
    size = kept.shape[1]
    far = max(offsets)
    panel, step = pl.program_id(0), pl.program_id(1)
    begin = sends_of[0] * SEND if sends_of else 0
    start = low - carry
    wide = size // TW

    @pl.when((panel == 0) & (step == 0))
    def _():
        for side in range(2):
            at = 0
            for ref in sends[side]:
                stores[side][at : at + ref.shape[0]] = ref[...]
                at += ref.shape[0]

    @pl.when(step == 0)
    def _():
        def row_of(slot):
            return place[2 + slot] * depth // TW

        totals = {}
        firsts = {}
        for slot, offset in enumerate(offsets[:high]):
            flags = [b_mask[row_of(slot), place[1] * tiles + j] for j in range(tiles)]
            firsts[offset] = sum(flags[:wide])
            totals[offset] = firsts[offset] + sum(flags[wide:])
        waiting = jnp.int32(0)
        leftover = []
        for slot in range(start, high):
            rows = slice((slot - start) * depth, (slot - start + 1) * depth)
            offset = offsets[slot]
            flags = [b_mask[row_of(slot), place[1] * tiles + panel * wide + j] for j in range(wide)]
            if offset == 0:
                for j in range(wide):
                    columns = pl.ds(pl.multiple_of(panel * size + j * TW, TW), TW)
                    kept[rows, j * TW : (j + 1) * TW] = own_ref[:, columns] * flags[j].astype(kept.dtype)
                continue
            total = totals[offset]
            begins = {}
            for sign in (-1, 1):
                begins[sign] = sum(
                    (jnp.maximum(totals[sign * hop], 2 * SEND) for hop in range(1, abs(offset))), jnp.int32(0)
                )
            before = panel * firsts[offset]
            for j, flag in enumerate(flags):
                at = (begins[-1] + before, begins[1] + total - 1 - before)
                columns = slice(j * TW, (j + 1) * TW)
                if offset == far:
                    on_right = at[0] < cap
                    for side, take in ((0, on_right), (1, jnp.logical_not(on_right))):
                        index = jnp.clip(at[side] - begin, 0, stores[side].shape[0] - 1)

                        @pl.when(take)
                        def _():
                            kept[rows, columns] = stores[side][index] * flag.astype(kept.dtype)
                else:
                    side = 0 if offset < 0 else 1
                    valid = flag
                    index = jnp.clip(at[side] - begin, 0, stores[side].shape[0] - 1)
                    if slot < low:
                        valid = jnp.where(at[side] >= carried, flag, 0)
                        waiting += valid
                        leftover.append((rows, columns, side, index, valid))
                    else:
                        if limit is not None:
                            valid = jnp.where(at[side] < limit, flag, 0)
                        kept[rows, columns] = stores[side][index] * valid.astype(kept.dtype)
                before += flag
        late[0] = waiting
        if carry:

            @pl.when(waiting != 0)
            def _():
                for rows, columns, side, index, valid in leftover:
                    kept[rows, columns] = stores[side][index] * valid.astype(kept.dtype)


    height = a_ref.shape[1]
    row_count = height // STEPS_OF[final]

    def total_of(from_slot):
        for r in range(0, row_count, PIECE[0]):
            inner = pl.ds(pl.multiple_of(step * row_count + r, PIECE[0]), PIECE[0])
            parts = [a_ref[slot, inner, :] for slot in range(from_slot, high)]
            parts = jnp.concatenate(parts, axis=1) if len(parts) > 1 else parts[0]
            for c in range(0, size, PIECE[1]):
                across = pl.ds(pl.multiple_of(panel * size + c, PIECE[1]), PIECE[1])
                product = jnp.dot(
                    parts, kept[(from_slot - start) * depth :, c : c + PIECE[1]], preferred_element_type=jnp.float32
                )
                base = base_ref[r : r + PIECE[0], c : c + PIECE[1]] if low == 0 else base_ref[inner, across]
                total = base.astype(jnp.float32) + product
                if final:
                    done[inner, across] = total.astype(done.dtype)
                else:
                    out_ref[inner, across] = total
            if final:
                across = pl.ds(pl.multiple_of(panel * size, size), size)
                pltpu.make_async_copy(done.at[inner, across], out_ref.at[inner, across], written).start()

    if carry:

        @pl.when(late[0] != 0)
        def _():
            total_of(start)

        @pl.when(late[0] == 0)
        def _():
            total_of(low)

    else:
        total_of(low)

    if final:

        @pl.when((panel == pl.num_programs(0) - 1) & (step == pl.num_programs(1) - 1))
        def _():
            pltpu.make_async_copy(done, out_ref, written).wait()


def gather_multiply(
    place, b_mask, a_kept, own, sends, base, *, low, high, carry, carried, limit, offsets, sends_of, cap, width
):
    height, depth = a_kept.shape[1:]
    final = high == len(offsets)
    size = width // 2
    steps = STEPS_OF[final]
    rows = height // steps
    whole = pl.BlockSpec(memory_space=pltpu.VMEM)
    block = pl.BlockSpec((rows, size), lambda p, i, *_: (i, p))
    operands = [place, b_mask, a_kept]
    in_specs = [whole]
    if own is not None:
        operands.append(own)
        in_specs.append(whole)
    for side in range(2):
        arrays = [sends[index][side] for index in sends_of]
        operands += arrays
        in_specs += [whole] * len(arrays)
    store = pltpu.VMEM((max(1, sum(array.shape[0] for array in arrays)), depth, TW), jnp.bfloat16)
    operands.append(base)
    in_specs.append(whole if low else block)
    aliases = {}
    if final:
        out_shape = jax.ShapeDtypeStruct((height, width), jnp.bfloat16)
    else:
        out_shape = pltpu.VMEM((height, width), jnp.float32)
        if low:
            aliases = {len(operands) - 1: 0}
    return pl.pallas_call(
        functools.partial(
            gather_multiply_body, low=low, high=high, carry=carry, carried=carried, limit=limit, offsets=offsets,
            sends_of=sends_of, tiles=width // TW, cap=cap, own=own is not None, final=final,
        ),
        grid_spec=pltpu.PrefetchScalarGridSpec(
            num_scalar_prefetch=2,
            grid=(2, steps),
            in_specs=in_specs,
            out_specs=pl.BlockSpec(memory_space=pl.ANY) if final else whole,
            scratch_shapes=[
                pltpu.VMEM(((high - low + carry) * depth, size), jnp.bfloat16), store, store, pltpu.SMEM((1,), jnp.int32)
            ]
            + ([pltpu.VMEM((height, width), jnp.bfloat16), pltpu.SemaphoreType.DMA] if final else []),
        ),
        out_shape=out_shape,
        input_output_aliases=aliases,
        cost_estimate=pl.CostEstimate(flops=height * size * depth // 16, bytes_accessed=height * size // 16, transcendentals=0),
        compiler_params=pltpu.CompilerParams(vmem_limit_bytes=GATHER_VMEM),
    )(*operands)


def sparse(n, cap, a_tiles, b_tiles, a_mask, b_mask, c_given, plan, *heads):
    ring = ring_of(n)
    right = [(ring[i], ring[(i + 1) % n]) for i in range(n)]
    left = [(t, s) for s, t in right]
    height, width = c_given.shape
    far = n // 2
    panel = width // 2
    tiles = width // TW
    offsets, place = places(n, lax.axis_index("row"), lax.axis_index("col"), height)

    sizes = [SEND] * (cap // SEND) + ([cap % SEND] if cap % SEND else [])
    last = len(sizes)

    def sent_by(count):
        return min(-(-count // SEND), last)

    cut = 1 + 2 * ((far - 1) // 2)
    near, edge = 2 * far - 3, 2 * far - 1
    middle = (sent_by(tiles * (far - 2)) - 1) * SEND
    limit = (cap - 2) // SEND * SEND
    phases = [
        dict(low=0, high=1, carry=0, carried=0, limit=None, sends_of=()),
        dict(low=1, high=cut, carry=0, carried=0, limit=None, sends_of=(0, sent_by(tiles * (cut // 2)))),
        dict(low=cut, high=near, carry=0, carried=0, limit=middle, sends_of=(2 * (cut // 2), middle // SEND)),
        dict(
            low=near, high=edge, carry=near - cut, carried=middle, limit=limit,
            sends_of=(min(2 * (far - 2), middle // SEND), limit // SEND),
        ),
        dict(
            low=edge, high=n, carry=edge - near, carried=limit, limit=None,
            sends_of=(min(2 * (far - 1), limit // SEND), last),
        ),
    ]
    work = collections.defaultdict(list)
    for phase in phases:
        begin, end = phase["sends_of"] or (0, 2)
        phase["sends_of"] = tuple(range(begin, end)) if phase["low"] else ()
        work[min(end + 1, last)].append(phase)

    sends = []
    tied = []
    other = a_kept = total = None
    for index in range(last + 1):
        if index < last:
            if index == 0:
                sources = heads
            elif index == 1:
                packed = pack(b_mask, b_tiles, n, False)
                sources = packed[::2]
            else:
                arrays = []
                for side in range(2):
                    arrays += [packed[2 * side + 1] if index == 2 else sends[index - 3][side], sends[index - 2][side]]
                if tied:
                    *arrays, _ = lax.optimization_barrier((*arrays, tied))
                    tied = []
                sources = choose(plan, arrays, sizes[index])
            sends.append([lax.ppermute(source, "row", pairs) for source, pairs in zip(sources, (right, left))])
        if index == 0:
            other = lax.ppermute(a_tiles, "col", [(0, 1), (1, 0)])
        if index == 1:
            source = pltpu.with_memory_space_constraint(a_tiles, pltpu.HBM)
            a_kept = prepare(place, a_mask, source, other, n)
            tied.append(a_kept)
        for phase in work[index]:
            first = phase["low"] == 0
            total = gather_multiply(
                place, b_mask, a_kept, b_tiles if first else None, sends,
                pltpu.with_memory_space_constraint(c_given, pltpu.HBM) if first else total,
                offsets=tuple(offsets), cap=cap, width=width, **phase,
            )
            tied.append(total)
    return total


def on_device(n, *args):
    b_tiles, b_mask = args[1], args[3]
    *heads, plan = pack(b_mask, b_tiles, n, True)
    tiles = b_tiles.shape[1] // TW
    most = tiles * (n // 2 - 1) + tiles // 2
    caps = [most - most * saved // 28 for saved in (4, 3)]
    branches = [functools.partial(sparse, n, cap) for cap in caps]
    branches.append(lambda *operands: dense(n, *operands[:5]))
    which = sum((plan[0] > cap).astype(jnp.int32) for cap in caps)
    return lax.switch(which, branches, *args, plan, *heads)


def solution(mesh):
    return jax.shard_map(
        functools.partial(on_device, mesh.shape["row"]),
        mesh=mesh,
        in_specs=(
            P(("grp", "row"), "col"),
            P(("grp", "row"), "col"),
            P("grp", None),
            P("grp", None),
            P(("grp", "row"), "col"),
        ),
        out_specs=P(("grp", "row"), "col"),
        check_vma=False,
    )
```
